32 devices in a mesh: section: 2 (over core), dp: 16 (over z, y, x).
Axes of the slice: x: 2, y: 2, z: 4, core: 2. Of those that a mesh axis runs over, the one named last changes fastest.
Arguments:
- tokens: bfloat16 [2, 1024, 768], P(None, 'dp'), may hold values from -6 to 6
- out_grad: bfloat16 [2, 1024, 768], P(None, 'dp'), may hold values from -6 to 6
- routes: int32 [2, 2, 1024, 1], P('section', None, 'dp'), may hold values from 0 to 3; in each aligned block of 64 rows (0 to 63, 64 to 127, ..., all dimensions but the last counted through in order) at most 24 rows name the same one
- doc_lengths: int32 [2, 16, 2], P(None, 'dp'), may hold values from 1 to 48, 64 in all within a row
- norm_attn: bfloat16 [2, 768], P('section', 'dp'), may hold values from 0.25 to 1.75
- attn_qkv: bfloat16 [2, 768, 2304], P('section', 'dp'), may hold values from -0.21875 to 0.21875
- rel_bias: bfloat16 [2, 384], P('section', 'dp'), may hold values from -4 to 4
- attn_out: bfloat16 [2, 768, 768], P('section', 'dp'), may hold values from -0.875 to 0.875
- norm_ffn: bfloat16 [2, 768], P('section', 'dp'), may hold values from 0.25 to 1.75
- router: bfloat16 [2, 768, 4], P('section', 'dp'), may hold values from -0.109375 to 0.109375
- expert_in: bfloat16 [2, 16, 768, 768], P('section', 'dp'), may hold values from -0.21875 to 0.21875
- expert_out: bfloat16 [2, 16, 768, 768], P('section', 'dp'), may hold values from -0.4375 to 0.4375
Outputs:
- layer_outputs: bfloat16 [2, 2, 1024, 768], P('section', None, 'dp')
- layer_input_grads: float32 [2, 2, 1024, 768], P('section', None, 'dp')
- grad_norm_attn: float32 [2, 768], P('section', 'dp')
- grad_attn_qkv: float32 [2, 768, 2304], P('section', 'dp')
- grad_rel_bias: float32 [2, 384], P('section', 'dp')
- grad_attn_out: float32 [2, 768, 768], P('section', 'dp')
- grad_norm_ffn: float32 [2, 768], P('section', 'dp')
- grad_router: float32 [2, 768, 4], P('section', 'dp')
- grad_expert_in: float32 [2, 16, 768, 768], P('section', 'dp')
- grad_expert_out: float32 [2, 16, 768, 768], P('section', 'dp')
The draws below stay inside these ranges and needn't reach their ends.
Inputs may be any that keep to these rules, and one draw needn't show every extreme that they name: `routes`: in each layer and micro-batch the 64 rows of one device name each expert at most 24 times, a bound that some block reaches. `doc_lengths`: the 2 lengths of one device's share of a micro-batch sum to 64; neither is more than 48.
All inputs are finite; a program needn't handle non-finite values.
Results may differ from the reference program's by a relative error of at most 0.028.
Values may be sent and summed in bfloat16 or wider, within the bound.
A program may use at most 128 MiB of HBM per device.

```python
import math
import jax
import jax.numpy as jnp
import numpy as np
from jax import lax

D = 768
HEADS = 12
HD = 64
FF = 3072
BUCKETS = 32
SPLIT = 4
MB = 2
DOCS = 2
TOK_MB = 64
EXPERTS = 4
CAP = 24
DOC_MOST = 48
TOKENS = 1024
N_DP = 16


def level_of(key, dims, cuts, least, top_value):
    level, own = 1.0, jax.random.fold_in(key, 6)
    for dim, parts in cuts:
        steps = jnp.exp(jax.random.uniform(jax.random.fold_in(own, dim), (parts,), jnp.float32, least / len(cuts), top_value / len(cuts)))
        level = level * jnp.repeat(steps, dims[dim] // parts).reshape([-1 if axis == dim else 1 for axis in range(len(dims))])
    return level


def profile(amount, total, most, skew):
    portions = [(1 << 20) // math.isqrt(rank ** skew) + 1 for rank in range(2, amount + 1)]
    rest, given = total - most - (amount - 1), [1] * (amount - 1)
    while rest > 0:
        free = [i for i in range(amount - 1) if given[i] < most]
        whole, budget = sum([portions[i] for i in free]), rest
        for i in free:
            extra = min(most - given[i], max(1, budget * portions[i] // whole), rest)
            given[i] = given[i] + extra
            rest = rest - extra
    return np.array([most] + given)


def uneven(stream_key, count, total, limit, skew):
    if count == 2:
        one = jax.random.randint(stream_key, (), max(1, total - limit), min(limit, total - 1) + 1)
        return jnp.stack([one, total - one])
    sizes = jnp.asarray(profile(count, total, limit, skew), jnp.int32)
    couples = (count - 1) // 2
    source_of, sink = sizes[1:1 + 2 * couples:2], sizes[2:2 + 2 * couples:2]
    slack = jnp.minimum(source_of - 1, limit - sink)
    passed = jax.random.randint(jax.random.fold_in(stream_key, 1), (couples,), 0, 1 << 20) % (slack + 1)
    sizes = sizes.at[1:1 + 2 * couples:2].set(source_of - passed).at[2:2 + 2 * couples:2].set(sink + passed)
    return sizes[jax.random.permutation(jax.random.fold_in(stream_key, 2), count)]


def assign_block(key, own, number, rows, number_of, top, limit, skew):
    order = jax.random.permutation(key, number_of)
    heavy_load, usual = load_shares(number_of, rows * top, limit, skew, True), load_shares(number_of, rows * top, limit, skew, False)
    places = jnp.arange(number_of)

    def named(tallies, rotation):
        used = int((tallies > 0).sum())
        fixed = max(1, used // 4)
        moved = fixed + (places - fixed + rotation * (used - fixed)) % max(1, number_of - fixed)
        return jnp.zeros((number_of,), jnp.int32).at[order[jnp.where(places < fixed, places, moved)]].set(jnp.asarray(tallies, jnp.int32))

    tallies = jnp.where(number % 4 == 0, named(heavy_load, number // 4), named(usual, number - number // 4 - 1))
    mixed = jax.random.permutation(jax.random.fold_in(own, 3), number_of)
    donor, taker = mixed[0:number_of // 2 * 2:2], mixed[1:number_of // 2 * 2:2]
    slack = jnp.minimum(tallies[donor] - 1, limit - tallies[taker]) // 2
    slack = jnp.where((donor == order[0]) | (taker == order[0]) | (tallies[taker] == 0), 0, jnp.maximum(slack, 0))
    moved = jax.random.randint(jax.random.fold_in(own, 4), (number_of // 2,), 0, 1 << 20) % (slack + 1)
    tallies = tallies.at[donor].add(-moved).at[taker].add(moved)
    members = jnp.searchsorted(jnp.cumsum(tallies), jnp.arange(rows * top), side="right").astype(jnp.int32)
    table = members.reshape(top, rows).T
    table = table[jax.random.permutation(jax.random.fold_in(own, 1), rows)]
    rotation = jax.random.randint(jax.random.fold_in(own, 2), (rows, 1), 0, top)
    return jnp.take_along_axis(table, (jnp.arange(top)[None, :] + rotation) % top, axis=1)


def load_shares(count, total, limit, skew, full):
    portions = [(1 << 20) // math.isqrt(grade ** skew) + 1 for grade in range(1, count + 1)]
    largest = limit if full else min(limit, max(-(-total // count), total * portions[0] // sum(portions)))
    least = 1 if total - largest >= count - 1 else 0
    given, surplus = [largest] + [least] * (count - 1), total - largest - least * (count - 1)
    while surplus > 0:
        free = [i for i in range(1, count) if given[i] < largest] or [i for i in range(1, count) if given[i] < limit]
        whole, remaining = sum([portions[i] for i in free]), surplus
        for i in free:
            extra = min(limit - given[i], max(1, remaining * portions[i] // whole), surplus)
            given[i] = given[i] + extra
            surplus = surplus - extra
    return np.array(given)


def scatter_about(key, dims, deviation, most, cuts=(), kind=jnp.bfloat16):
    drawn = jax.random.normal(key, dims, jnp.float32) * deviation
    if len(cuts) > 0:
        drawn = level_of(key, dims, cuts, -0.22, 0.18) * drawn
    return jnp.clip(drawn, min=-most, max=most).astype(kind)


def setup_inputs(seed: int = 0) -> dict:
    key_list = jax.random.split(jax.random.key(seed), 13)
    tokens = scatter_about(key_list[0], (MB, TOKENS, D), 1.0, 6.0, ((1, 16),))
    out_grad = scatter_about(key_list[1], (MB, TOKENS, D), 1.0, 6.0, ((1, 16),))
    routes_keys = jax.random.split(jax.random.fold_in(key_list[2], 1), 2 * MB * TOKENS // TOK_MB)
    routes_turns = jax.random.permutation(jax.random.fold_in(key_list[2], 3), 2 * MB * TOKENS // TOK_MB)
    routes = jax.vmap(lambda own, number: assign_block(jax.random.fold_in(key_list[2], 2), own, number, TOK_MB, EXPERTS, 1, CAP, 1))(routes_keys, routes_turns).reshape((2, MB, TOKENS, 1))
    doc_lengths = jax.vmap(lambda own: uneven(own, DOCS, TOK_MB, DOC_MOST, 2))(jax.random.split(key_list[3], MB * N_DP)).reshape((MB, N_DP, DOCS)).astype(jnp.int32)
    norm_attn = jnp.clip(1.0 + 0.15 * jax.random.normal(key_list[4], (2, D), jnp.float32), 0.25, 1.75).astype(jnp.bfloat16)
    attn_qkv = scatter_about(key_list[5], (2, D, 3 * D), D ** -0.5, 0.21875, ((0, 2), (1, 16)))
    rel_bias = scatter_about(key_list[6], (2, BUCKETS * HEADS), 1.0, 4.0, ((0, 2), (1, 16)))
    attn_out = scatter_about(key_list[7], (2, D, D), (D // 16) ** -0.5, 0.875, ((0, 2), (1, 16)))
    norm_ffn = jnp.clip(1.0 + 0.15 * jax.random.normal(key_list[8], (2, D), jnp.float32), 0.25, 1.75).astype(jnp.bfloat16)
    router = scatter_about(key_list[9], (2, D, EXPERTS), (4 * D) ** -0.5, 0.109375, ((0, 2), (1, 16)))
    expert_in = scatter_about(key_list[10], (2, EXPERTS * SPLIT, D, FF // SPLIT), D ** -0.5, 0.21875, ((0, 2), (1, 16)))
    expert_out = scatter_about(key_list[11], (2, EXPERTS * SPLIT, FF // SPLIT, D), (max(1, FF // (EXPERTS * EXPERTS))) ** -0.5, 0.4375, ((0, 2), (1, 16)))
    return dict(tokens=tokens, out_grad=out_grad, routes=routes, doc_lengths=doc_lengths, norm_attn=norm_attn, attn_qkv=attn_qkv, rel_bias=rel_bias, attn_out=attn_out, norm_ffn=norm_ffn, router=router, expert_in=expert_in, expert_out=expert_out)


@jax.custom_vjp
def low(v):
    return lax.optimization_barrier(v.astype(jnp.bfloat16)).astype(jnp.float32)

@jax.custom_vjp
def low_back(v):
    return v

def low_keep(v):
    return (low(v), None)

def low_pass(kept, grad):
    return (grad,)

def back_keep(v):
    return (v, None)

def back_low(kept, grad):
    return (low(grad),)
low.defvjp(low_keep, low_pass)
low_back.defvjp(back_keep, back_low)
EPSILON = 1e-06
HIGHEST = lax.Precision.HIGHEST
far_limits = np.array([8, 12, 16, 23, 32, 46, 64, 91], dtype=np.int32)

def buckets_of(row_count):
    places = jnp.arange(row_count, dtype=jnp.int32)
    offset = places[None, :] - places[:, None]
    distance = jnp.abs(offset).astype(jnp.int32)
    beyond = lax.optimization_barrier(jnp.sum((distance[:, :, None] >= jnp.asarray(far_limits)[None, None, :]).astype(jnp.int32), axis=-1)).astype(jnp.int32)
    nearby = jnp.where(distance < 8, distance, 7 + beyond).astype(jnp.int32)
    upward = jnp.where(offset > 0, BUCKETS // 2, 0).astype(jnp.int32)
    return (nearby + upward).astype(jnp.int32)

def documents_of(lengths, row_count):
    ending = jnp.cumsum(lengths, axis=-1).astype(jnp.int32)
    places = jnp.arange(row_count, dtype=jnp.int32)
    return lax.optimization_barrier(jnp.sum((places[:, None] >= ending[..., None, :]).astype(jnp.int32), axis=-1)).astype(jnp.int32)

def slot_table(target_row):
    empty = jnp.full((EXPERTS * CAP,), TOK_MB, jnp.int32)
    return empty.at[target_row].set(jnp.arange(TOK_MB, dtype=jnp.int32))

def take_rows(table_rows, index_rows):
    return table_rows[index_rows]

def expert_apply(packed):
    token_rows, weight_in, weight_back = packed
    copies = low_back(jnp.broadcast_to(token_rows[None], (SPLIT,) + token_rows.shape))
    hidden = low_back(jnp.einsum('kmrd,kdf->kmrf', copies, weight_in, precision=HIGHEST))
    active = low(jax.nn.gelu(hidden, approximate=True))
    pieces = low(low_back(jnp.einsum('kmrf,kfd->kmrd', active, weight_back, precision=HIGHEST)))
    return lax.optimization_barrier(jnp.sum(pieces, axis=0))

def encoder_layer(layer_in, gain_one, w_qkv, table, w_out, gain_two, w_route, weight_in, weight_back, route_rows, lengths):
    block_count = layer_in.shape[0]
    scale_one = lax.rsqrt(lax.optimization_barrier(jnp.mean(layer_in * layer_in, axis=-1, keepdims=True)) + EPSILON)
    normed = low(layer_in * scale_one * gain_one)
    qkv_rows = low(low_back(jnp.einsum('btd,de->bte', normed, w_qkv, precision=HIGHEST)))
    query_heads = qkv_rows[..., :D].reshape(block_count, TOK_MB, HEADS, HD)
    key_heads = qkv_rows[..., D:2 * D].reshape(block_count, TOK_MB, HEADS, HD)
    value_heads = qkv_rows[..., 2 * D:].reshape(block_count, TOK_MB, HEADS, HD)
    score_bias = jnp.transpose(table.reshape(BUCKETS, HEADS)[buckets_of(TOK_MB)], (2, 0, 1))
    documents = documents_of(lengths, TOK_MB)
    same_doc = documents[:, :, None] == documents[:, None, :]
    scores = jnp.einsum('bthd,bshd->bhts', query_heads, key_heads, precision=HIGHEST) * (1.0 / math.sqrt(HD)) + score_bias[None]
    scores = low_back(jnp.where(same_doc[:, None], scores, -1000000000.0))
    soft_rows = jax.nn.softmax(scores, axis=-1)
    attended = jnp.einsum('bhts,bshd->bthd', low(soft_rows), value_heads, precision=HIGHEST).reshape(block_count, TOK_MB, D)
    attended = low(low_back(attended))
    middle = layer_in + low_back(jnp.einsum('btd,de->bte', attended, w_out, precision=HIGHEST))
    scale_two = lax.rsqrt(lax.optimization_barrier(jnp.mean(middle * middle, axis=-1, keepdims=True)) + EPSILON)
    routed = low(middle * scale_two * gain_two)
    logits = low_back(jnp.einsum('btd,de->bte', routed, w_route, precision=HIGHEST))
    choice_prob = jax.nn.softmax(logits, axis=-1)
    picked = (route_rows[..., None] == jnp.arange(EXPERTS, dtype=jnp.int32)).astype(jnp.int32)
    gate_prob = lax.optimization_barrier(jnp.sum(choice_prob * picked.astype(jnp.float32), axis=-1))
    ranks = lax.optimization_barrier(jnp.sum((jnp.cumsum(picked, axis=1).astype(jnp.int32) - 1) * picked, axis=-1)).astype(jnp.int32)
    target = (route_rows * CAP + ranks).astype(jnp.int32)
    source = jax.vmap(slot_table)(target)
    padded = jnp.concatenate([routed, jnp.zeros((block_count, 1, D), jnp.float32)], axis=1)
    gathered = jax.vmap(take_rows)(padded, source)
    grouped = gathered.reshape(MB, N_DP, EXPERTS, CAP, D).transpose(2, 0, 1, 3, 4).reshape(EXPERTS, MB, N_DP * CAP, D)
    inward = weight_in.reshape(EXPERTS, SPLIT, D, FF // SPLIT)
    outward = weight_back.reshape(EXPERTS, SPLIT, FF // SPLIT, D)
    expert_rows = lax.map(jax.checkpoint(expert_apply), (grouped, inward, outward))
    spread = expert_rows.reshape(EXPERTS, MB, N_DP, CAP, D).transpose(1, 2, 0, 3, 4).reshape(block_count, EXPERTS * CAP, D)
    returned = jax.vmap(take_rows)(spread, target)
    return middle + gate_prob[..., None] * returned

def reference(tokens, out_grad, routes, doc_lengths, norm_attn, attn_qkv, rel_bias, attn_out, norm_ffn, router, expert_in, expert_out):
    weights = tuple((member.astype(jnp.float32) for member in (norm_attn, attn_qkv, rel_bias, attn_out, norm_ffn, router, expert_in, expert_out)))
    start_rows = tokens.astype(jnp.float32).reshape(MB * N_DP, TOK_MB, D)
    lengths = doc_lengths.reshape(MB * N_DP, DOCS)
    route_rows = routes.reshape(2, MB * N_DP, TOK_MB)

    def forward(first_in, handed_extra, params):
        first_out = encoder_layer(first_in, *[member[0] for member in params], route_rows[0], lengths)
        handed = low(low_back(first_out)) + handed_extra
        second_out = encoder_layer(handed, *[member[1] for member in params], route_rows[1], lengths)
        return (second_out, first_out)
    handed_zero = jnp.zeros_like(start_rows)
    second_out, pull_back, first_out = jax.vjp(forward, start_rows, handed_zero, weights, has_aux=True)
    cotangent = out_grad.astype(jnp.float32).reshape(MB * N_DP, TOK_MB, D)
    start_grad, handed_grad, weight_grads = pull_back(cotangent)
    outputs = jnp.stack([first_out, second_out]).astype(jnp.bfloat16).reshape(2, MB, TOK_MB * N_DP, D)
    input_grads = jnp.stack([start_grad, handed_grad]).reshape(2, MB, TOK_MB * N_DP, D)
    return (outputs, input_grads, weight_grads[0], weight_grads[1], weight_grads[2], weight_grads[3], weight_grads[4], weight_grads[5], weight_grads[6], weight_grads[7])
```

```python
import math

import jax
import jax.numpy as jnp
import numpy as np
from jax import lax
from jax.sharding import PartitionSpec as P

HEADS = 12
HD = 64
BUCKETS = 32
SPLIT = 4


EPSILON = 1e-06
far_limits = np.array([8, 12, 16, 23, 32, 46, 64, 91], dtype=np.int32)


def buckets_of(row_count):
    places = jnp.arange(row_count, dtype=jnp.int32)
    offset = places[None, :] - places[:, None]
    distance = jnp.abs(offset)
    beyond = jnp.sum(
        (distance[:, :, None] >= jnp.asarray(far_limits)[None, None, :]).astype(jnp.int32), axis=-1
    )
    nearby = jnp.where(distance < 8, distance, 7 + beyond)
    upward = jnp.where(offset > 0, BUCKETS // 2, 0).astype(jnp.int32)
    return nearby + upward


def documents_of(lengths, row_count):
    ending = jnp.cumsum(lengths, axis=-1)
    places = jnp.arange(row_count, dtype=jnp.int32)
    return jnp.sum((places[:, None] >= ending[..., None, :]).astype(jnp.int32), axis=-1)


def same_of(lengths, row_count):
    documents = documents_of(lengths, row_count)
    return documents[:, None] == documents[None, :]


def picks_of(row_count):
    return (
        buckets_of(row_count)[:, :, None] == jnp.arange(BUCKETS, dtype=jnp.int32)[None, None, :]
    ).astype(jnp.bfloat16)


def bias_of(table, row_count):
    bucket_picks = picks_of(row_count)
    score_bias = jnp.einsum(
        "tsb,bh->hts",
        bucket_picks,
        table.reshape(BUCKETS, HEADS),
        preferred_element_type=jnp.float32,
    )
    return (score_bias, bucket_picks)


def split_heads(qkv_rows):
    row_count = qkv_rows.shape[0]
    model_width = qkv_rows.shape[1] // 3
    query_heads = qkv_rows[:, :model_width].reshape(row_count, HEADS, HD)
    key_heads = qkv_rows[:, model_width : 2 * model_width].reshape(row_count, HEADS, HD)
    value_heads = qkv_rows[:, 2 * model_width :].reshape(row_count, HEADS, HD)
    return (query_heads, key_heads, value_heads)


def scores_of(query_heads, key_heads, score_bias, same_doc):
    raw_scores = (
        jnp.einsum("thd,shd->hts", query_heads, key_heads, preferred_element_type=jnp.float32)
        * (1.0 / math.sqrt(HD))
        + score_bias
    )
    return jnp.where(same_doc[None], raw_scores, -1000000000.0)


def placement_of(route_now, expert_count, slot_count):
    row_count = route_now.shape[0]
    places = jnp.arange(row_count, dtype=jnp.int32)
    earlier = (route_now[:, None] == route_now[None, :]) & (places[None, :] < places[:, None])
    ranks = jnp.sum(earlier.astype(jnp.int32), axis=1)
    target = route_now * slot_count + ranks
    flat = (
        jnp.arange(expert_count * slot_count, dtype=jnp.int32)[:, None] == target[None, :]
    ).astype(jnp.bfloat16)
    return flat.reshape(expert_count, slot_count, row_count)


def spread_copies(select, token_rows, dp_count):
    expert_count = select.shape[0]
    slot_count = select.shape[1]
    model_width = token_rows.shape[1]
    grouped = jnp.einsum(
        "ect,td->ecd", select, token_rows, preferred_element_type=jnp.float32
    ).astype(jnp.bfloat16)
    copies = jnp.broadcast_to(grouped[:, None], (expert_count, SPLIT, slot_count, model_width))
    return copies.reshape(dp_count, slot_count, model_width)


def rms_back(grad_rows, inputs, scale_rows):
    normal_rows = inputs * scale_rows
    return scale_rows * (
        grad_rows - normal_rows * jnp.mean(grad_rows * normal_rows, axis=-1, keepdims=True)
    )


def smooth(values):
    return jax.nn.gelu(values, approximate=True)


def layer_forward(layer_in, weights, route_now, lengths, weight_in, weight_back):
    gain_one, w_qkv, table, w_out, gain_two, w_route = weights
    row_count, model_width = layer_in.shape
    dp_count = lax.axis_size("dp")
    expert_count = w_route.shape[1]
    slot_count = 3 * row_count * SPLIT // (2 * dp_count)
    scale_one = lax.rsqrt(jnp.mean(layer_in * layer_in, axis=-1, keepdims=True) + EPSILON)
    normed = (layer_in * scale_one * gain_one.astype(jnp.float32)).astype(jnp.bfloat16)
    qkv_rows = jnp.dot(normed, w_qkv, preferred_element_type=jnp.float32).astype(jnp.bfloat16)
    query_heads, key_heads, value_heads = split_heads(qkv_rows)
    score_bias, bucket_picks = bias_of(table, row_count)
    same_doc = same_of(lengths, row_count)
    scores = scores_of(query_heads, key_heads, score_bias, same_doc)
    row_max = jnp.max(scores, axis=-1, keepdims=True)
    exp_rows = jnp.exp(scores - row_max)
    exp_total = jnp.sum(exp_rows, axis=-1, keepdims=True)
    soft_rows = exp_rows / exp_total
    soft_low = soft_rows.astype(jnp.bfloat16)
    attended = jnp.einsum("hts,shd->thd", soft_low, value_heads, preferred_element_type=jnp.float32)
    attended = attended.reshape(row_count, model_width).astype(jnp.bfloat16)
    middle = layer_in + jnp.dot(attended, w_out, preferred_element_type=jnp.float32)
    scale_two = lax.rsqrt(jnp.mean(middle * middle, axis=-1, keepdims=True) + EPSILON)
    routed = (middle * scale_two * gain_two.astype(jnp.float32)).astype(jnp.bfloat16)
    logits = jnp.dot(routed, w_route, preferred_element_type=jnp.float32)
    choice_prob = jax.nn.softmax(logits, axis=-1)
    picked = (route_now[:, None] == jnp.arange(expert_count, dtype=jnp.int32)[None, :]).astype(
        jnp.float32
    )
    gate_prob = jnp.sum(choice_prob * picked, axis=-1)
    select = placement_of(route_now, expert_count, slot_count)
    outgoing = spread_copies(select, routed, dp_count)
    arrived = lax.all_to_all(outgoing, "dp", split_axis=0, concat_axis=0, tiled=True)
    token_rows = arrived.reshape(-1, model_width)
    hidden = jnp.dot(token_rows, weight_in, preferred_element_type=jnp.float32)
    active = smooth(hidden).astype(jnp.bfloat16)
    partial_out = (
        jnp.dot(active, weight_back, preferred_element_type=jnp.float32)
        .astype(jnp.bfloat16)
        .reshape(arrived.shape)
    )
    coming_back = lax.all_to_all(partial_out, "dp", split_axis=0, concat_axis=0, tiled=True)
    returned, hidden, arrived = (
        coming_back,
        hidden.reshape(arrived.shape[0], arrived.shape[1], -1),
        arrived,
    )
    combined = jnp.einsum(
        "ekcd,ect->td",
        returned.reshape(expert_count, SPLIT, slot_count, model_width),
        select,
        preferred_element_type=jnp.float32,
    )
    result = middle + gate_prob[:, None] * combined
    kept_state = (
        layer_in,
        scale_one,
        normed,
        qkv_rows,
        soft_rows,
        attended,
        middle,
        scale_two,
        routed,
        choice_prob,
        gate_prob,
        combined,
        hidden,
        arrived,
    )
    return (result, kept_state)


def layer_backward(upstream, kept_state, weights, route_now, lengths, weight_in, weight_back):
    (
        layer_in,
        scale_one,
        normed,
        qkv_rows,
        soft_rows,
        attended,
        middle,
        scale_two,
        routed,
        choice_prob,
        gate_prob,
        combined,
        hidden,
        arrived,
    ) = kept_state
    gain_one, w_qkv, table, w_out, gain_two, w_route = weights
    row_count, model_width = layer_in.shape
    dp_count = lax.axis_size("dp")
    expert_count = w_route.shape[1]
    slot_count = 3 * row_count * SPLIT // (2 * dp_count)
    picked = (route_now[:, None] == jnp.arange(expert_count, dtype=jnp.int32)[None, :]).astype(
        jnp.float32
    )
    select = placement_of(route_now, expert_count, slot_count)
    down_grad = (gate_prob[:, None] * upstream).astype(jnp.bfloat16)
    gate_grad = jnp.sum(upstream * combined, axis=-1)
    logit_grad = (choice_prob * (picked - gate_prob[:, None]) * gate_grad[:, None]).astype(
        jnp.bfloat16
    )
    routed_grad = jnp.einsum("te,de->td", logit_grad, w_route, preferred_element_type=jnp.float32)
    outgoing = spread_copies(select, down_grad, dp_count)
    arrived_grad = lax.all_to_all(outgoing, "dp", split_axis=0, concat_axis=0, tiled=True)
    rows_grad = arrived_grad.reshape(-1, model_width)
    active_grad = jnp.einsum(
        "rd,fd->rf", rows_grad, weight_back, preferred_element_type=jnp.float32
    )
    hidden_rows = hidden.reshape(rows_grad.shape[0], -1)
    active_rows, smooth_pull = jax.vjp(smooth, hidden_rows)
    hidden_grad = smooth_pull(active_grad)[0].astype(jnp.bfloat16)
    active_low = active_rows.astype(jnp.bfloat16)
    arrived_rows = arrived.reshape(-1, model_width)
    copy_grad = jnp.einsum(
        "rf,df->rd", hidden_grad, weight_in, preferred_element_type=jnp.float32
    ).astype(jnp.bfloat16)
    copy_back = lax.all_to_all(
        copy_grad.reshape(dp_count, slot_count, model_width),
        "dp",
        split_axis=0,
        concat_axis=0,
        tiled=True,
    )
    routed_grad = routed_grad + jnp.einsum(
        "ekcd,ect->td",
        copy_back.reshape(expert_count, SPLIT, slot_count, model_width),
        select,
        preferred_element_type=jnp.float32,
    )
    gain_two_grad = jnp.sum(routed_grad * middle * scale_two, axis=0)
    middle_grad = upstream + rms_back(routed_grad * gain_two.astype(jnp.float32), middle, scale_two)
    branch_grad = middle_grad.astype(jnp.bfloat16)
    attended_grad = jnp.einsum(
        "te,de->td", branch_grad, w_out, preferred_element_type=jnp.float32
    ).astype(jnp.bfloat16)
    attended_grad = attended_grad.reshape(row_count, HEADS, HD)
    query_heads, key_heads, value_heads = split_heads(qkv_rows)
    bucket_picks = picks_of(row_count)
    value_grad = jnp.einsum(
        "hts,thd->shd",
        soft_rows.astype(jnp.bfloat16),
        attended_grad,
        preferred_element_type=jnp.float32,
    )
    prob_grad = jnp.einsum(
        "thd,shd->hts", attended_grad, value_heads, preferred_element_type=jnp.float32
    )
    score_grad = (
        soft_rows * (prob_grad - jnp.sum(soft_rows * prob_grad, axis=-1, keepdims=True))
    ).astype(jnp.bfloat16)
    query_grad = jnp.einsum(
        "hts,shd->thd", score_grad, key_heads, preferred_element_type=jnp.float32
    ) * (1.0 / math.sqrt(HD))
    key_grad = jnp.einsum(
        "hts,thd->shd", score_grad, query_heads, preferred_element_type=jnp.float32
    ) * (1.0 / math.sqrt(HD))
    table_grad = jnp.einsum(
        "tsb,hts->bh", bucket_picks, score_grad, preferred_element_type=jnp.float32
    ).reshape(-1)
    qkv_grad = jnp.concatenate(
        [
            query_grad.reshape(row_count, model_width),
            key_grad.reshape(row_count, model_width),
            value_grad.reshape(row_count, model_width),
        ],
        axis=1,
    ).astype(jnp.bfloat16)
    normed_grad = jnp.einsum("te,de->td", qkv_grad, w_qkv, preferred_element_type=jnp.float32)
    gain_one_grad = jnp.sum(normed_grad * layer_in * scale_one, axis=0)
    input_grad = middle_grad + rms_back(
        normed_grad * gain_one.astype(jnp.float32), layer_in, scale_one
    )
    small_grads = (gain_one_grad, table_grad, gain_two_grad)
    factor_rows = (normed, qkv_grad, attended, branch_grad, routed, logit_grad)
    expert_rows = (arrived_rows, hidden_grad, active_low, rows_grad)
    return (input_grad, small_grads, factor_rows, expert_rows)


def shared_from(small_grads, factor_rows):
    normed, qkv_grad, attended, branch_grad, routed, logit_grad = factor_rows
    qkv_weight_grad = jnp.einsum("td,te->de", normed, qkv_grad, preferred_element_type=jnp.float32)
    out_weight_grad = jnp.einsum(
        "td,te->de", attended, branch_grad, preferred_element_type=jnp.float32
    )
    route_weight_grad = jnp.einsum(
        "td,te->de", routed, logit_grad, preferred_element_type=jnp.float32
    )
    return (
        small_grads[0],
        qkv_weight_grad,
        small_grads[1],
        out_weight_grad,
        small_grads[2],
        route_weight_grad,
    )


SMALL = 256


def swap_cores(block):
    return lax.ppermute(block, "section", [(0, 1), (1, 0)])


def per_core(section_index, first_one, second_one):
    return jnp.where(section_index == 0, first_one, second_one)


def pack_columns(wide, square, columns):
    small = jnp.concatenate(columns, axis=1)
    small = jnp.pad(small, ((0, 0), (0, SMALL - small.shape[1])))
    return jnp.concatenate([wide, square, small], axis=1)


def spaced(table, group_count):
    table = table.reshape(group_count, -1)
    row_share = 2 * table.shape[1]
    return jnp.pad(table, ((0, 0), (0, row_share - table.shape[1]))).reshape(-1, 1)


def gather_rows(shard):
    dp_count = lax.axis_size("dp")
    copies = jnp.broadcast_to(shard[None], (dp_count,) + shard.shape)
    got = lax.all_to_all(copies, "dp", split_axis=0, concat_axis=0, tiled=True)
    return got.reshape(dp_count * shard.shape[0], shard.shape[1])


def sum_rows(whole):
    dp_count = lax.axis_size("dp")
    parts = whole.reshape(dp_count, whole.shape[0] // dp_count, whole.shape[1])
    got = lax.all_to_all(parts, "dp", split_axis=0, concat_axis=0, tiled=True)
    return jnp.sum(got.astype(jnp.float32), axis=0)


def unpack_weights(packed, width, expert_count):
    dp_count = lax.axis_size("dp")
    small = packed[:, 4 * width :]
    table = small[:, 2].reshape(dp_count, -1)
    table = table[:, : table.shape[1] // 2].reshape(-1)
    return (
        small[:, 0],
        packed[:, : 3 * width],
        table,
        packed[:, 3 * width : 4 * width],
        small[:, 1],
        small[:, 3 : 3 + expert_count],
    )


def shards(
    tokens,
    out_grad,
    routes,
    doc_lengths,
    norm_attn,
    attn_qkv,
    rel_bias,
    attn_out,
    norm_ffn,
    router,
    expert_in,
    expert_out,
):
    core = lax.axis_index("section")
    dp_count = lax.axis_size("dp")
    width = tokens.shape[2]
    expert_count = router.shape[2]
    own_pack = pack_columns(
        attn_qkv[0],
        attn_out[0],
        [norm_attn[0][:, None], norm_ffn[0][:, None], spaced(rel_bias[0], 1), router[0]],
    )
    half = own_pack.shape[1] // 2
    first_half, second_half = own_pack[:, :half], own_pack[:, half:]
    other_part = swap_cores(per_core(core, second_half, first_half))
    part_zero = per_core(core, first_half, other_part)
    part_one = per_core(core, other_part, second_half)

    def whole_of(part):
        mine = gather_rows(part)
        theirs = swap_cores(mine)
        packed = jnp.concatenate(
            [per_core(core, mine, theirs), per_core(core, theirs, mine)], axis=1
        )
        return unpack_weights(packed, width, expert_count)

    weights = [whole_of(part_zero), None]
    other_in = swap_cores(expert_in[0, 0])
    other_out = swap_cores(expert_out[0, 0])
    ins = [per_core(core, expert_in[0, 0], other_in), per_core(core, other_in, expert_in[0, 0])]
    outs = [
        per_core(core, expert_out[0, 0], other_out),
        per_core(core, other_out, expert_out[0, 0]),
    ]
    route_table = routes[0, :, :, 0]
    other_route = swap_cores(per_core(core, route_table[1], route_table[0]))
    own_route = per_core(core, route_table[0], route_table[1])
    route_rows = [
        per_core(core, own_route, other_route),
        per_core(core, other_route, own_route),
    ]
    lengths = per_core(core, doc_lengths[0, 0], doc_lengths[1, 0])
    layer_in = per_core(core, tokens[0], tokens[1]).astype(jnp.float32)
    weights[1] = whole_of(part_one)
    kept, lows = [], []
    for layer in range(2):
        result, state = layer_forward(
            layer_in, weights[layer], route_rows[layer], lengths, ins[layer], outs[layer]
        )
        low = result.astype(jnp.bfloat16)
        lows.append(low)
        kept.append(state)
        layer_in = low.astype(jnp.float32)

    def sorted_out(pair):
        mine = per_core(core, pair[0], pair[1])
        theirs = swap_cores(per_core(core, pair[1], pair[0]))
        return jnp.stack([per_core(core, mine, theirs), per_core(core, theirs, mine)])

    upstream = per_core(core, out_grad[0], out_grad[1]).astype(jnp.float32)
    input_grads, expert_rows, summed = [None, None], [None, None], [None, None]
    for layer in (1, 0):
        input_grad, small_grads, factor_rows, expert_rows[layer] = layer_backward(
            upstream,
            kept[layer],
            weights[layer],
            route_rows[layer],
            lengths,
            ins[layer],
            outs[layer],
        )
        input_grads[layer] = input_grad
        upstream = input_grad.astype(jnp.bfloat16).astype(jnp.float32)
        totals = shared_from(small_grads, factor_rows)
        packed = pack_columns(
            totals[1],
            totals[3],
            [totals[0][:, None], totals[4][:, None], spaced(totals[2], dp_count), totals[5]],
        ).astype(jnp.bfloat16)
        left, right = packed[:, :half], packed[:, half:]
        theirs = swap_cores(per_core(core, right, left))
        mine = per_core(core, left, right)
        both = (mine.astype(jnp.float32) + theirs.astype(jnp.float32)).astype(jnp.bfloat16)
        summed[layer] = sum_rows(both)

    def joined_rows(index):
        mine = per_core(core, expert_rows[0][index], expert_rows[1][index])
        theirs = swap_cores(per_core(core, expert_rows[1][index], expert_rows[0][index]))
        return jnp.concatenate([mine, theirs], axis=0)

    arrived_all, hidden_grad_all, active_all, rows_grad_all = [joined_rows(i) for i in range(4)]
    in_total = jnp.einsum(
        "rd,rf->df", arrived_all, hidden_grad_all, preferred_element_type=jnp.float32
    )
    back_total = jnp.einsum(
        "rf,rd->fd", active_all, rows_grad_all, preferred_element_type=jnp.float32
    )
    outputs = sorted_out(lows)
    input_store = sorted_out(input_grads)
    mine = per_core(core, summed[0], summed[1])
    theirs = swap_cores(per_core(core, summed[1], summed[0]))
    total = jnp.concatenate([per_core(core, mine, theirs), per_core(core, theirs, mine)], axis=1)
    small = total[:, 4 * width :]
    return (
        outputs[None],
        input_store[None],
        small[None, :, 0],
        total[None, :, : 3 * width],
        small[None, : rel_bias.shape[1], 2],
        total[None, :, 3 * width : 4 * width],
        small[None, :, 1],
        small[None, :, 3 : 3 + expert_count],
        in_total[None, None],
        back_total[None, None],
    )


def solution(mesh):
    placed = (
        P(None, "dp", None),
        P(None, "dp", None),
        P("section", None, "dp", None),
        P(None, "dp", None),
        P("section", "dp"),
        P("section", "dp", None),
        P("section", "dp"),
        P("section", "dp", None),
        P("section", "dp"),
        P("section", "dp", None),
        P("section", "dp", None, None),
        P("section", "dp", None, None),
    )
    return jax.shard_map(
        shards,
        mesh=mesh,
        in_specs=placed,
        out_specs=(
            P("section", None, "dp", None),
            P("section", None, "dp", None),
            P("section", "dp"),
            P("section", "dp", None),
            P("section", "dp"),
            P("section", "dp", None),
            P("section", "dp"),
            P("section", "dp", None),
            P("section", "dp", None, None),
            P("section", "dp", None, None),
        ),
        check_vma=False,
    )
```

```python
import math

import jax
import jax.numpy as jnp
import numpy as np
from jax import lax
from jax.experimental import pallas as pl
from jax.experimental.pallas import tpu as pltpu
from jax.sharding import PartitionSpec as P

HEADS = 12
HD = 64
BUCKETS = 32
SPLIT = 4


EPSILON = 1e-06
far_limits = np.array([8, 12, 16, 23, 32, 46, 64, 91], dtype=np.int32)


def buckets_of(row_count):
    places = jnp.arange(row_count, dtype=jnp.int32)
    offset = places[None, :] - places[:, None]
    distance = jnp.abs(offset)
    beyond = jnp.sum(
        (distance[:, :, None] >= jnp.asarray(far_limits)[None, None, :]).astype(jnp.int32), axis=-1
    )
    nearby = jnp.where(distance < 8, distance, 7 + beyond)
    upward = jnp.where(offset > 0, BUCKETS // 2, 0).astype(jnp.int32)
    return nearby + upward


def documents_of(lengths, row_count):
    ending = jnp.cumsum(lengths, axis=-1)
    places = jnp.arange(row_count, dtype=jnp.int32)
    return jnp.sum((places[:, None] >= ending[..., None, :]).astype(jnp.int32), axis=-1)


def same_of(lengths, row_count):
    documents = documents_of(lengths, row_count)
    return documents[:, None] == documents[None, :]


def picks_of(row_count):
    return (
        buckets_of(row_count)[:, :, None] == jnp.arange(BUCKETS, dtype=jnp.int32)[None, None, :]
    ).astype(jnp.bfloat16)


def bias_of(table, row_count):
    bucket_picks = picks_of(row_count)
    score_bias = jnp.einsum(
        "tsb,bh->hts",
        bucket_picks,
        table.reshape(BUCKETS, HEADS),
        preferred_element_type=jnp.float32,
    )
    return (score_bias, bucket_picks)


def split_heads(qkv_rows):
    row_count = qkv_rows.shape[0]
    model_width = qkv_rows.shape[1] // 3
    query_heads = qkv_rows[:, :model_width].reshape(row_count, HEADS, HD)
    key_heads = qkv_rows[:, model_width : 2 * model_width].reshape(row_count, HEADS, HD)
    value_heads = qkv_rows[:, 2 * model_width :].reshape(row_count, HEADS, HD)
    return (query_heads, key_heads, value_heads)


def scores_of(query_heads, key_heads, score_bias, same_doc):
    raw_scores = (
        jnp.einsum("thd,shd->hts", query_heads, key_heads, preferred_element_type=jnp.float32)
        * (1.0 / math.sqrt(HD))
        + score_bias
    )
    return jnp.where(same_doc[None], raw_scores, -1000000000.0)


def placement_of(route_now, expert_count, slot_count):
    row_count = route_now.shape[0]
    places = jnp.arange(row_count, dtype=jnp.int32)
    earlier = (route_now[:, None] == route_now[None, :]) & (places[None, :] < places[:, None])
    ranks = jnp.sum(earlier.astype(jnp.int32), axis=1)
    target = route_now * slot_count + ranks
    flat = (
        jnp.arange(expert_count * slot_count, dtype=jnp.int32)[:, None] == target[None, :]
    ).astype(jnp.bfloat16)
    return flat.reshape(expert_count, slot_count, row_count)


MESH = pl.DeviceIdType.MESH


def places_of(groups):
    core = lax.axis_index("section")
    me = lax.axis_index("dp")
    group, place = me // SPLIT, lax.rem(me, SPLIT)
    across = place + 1 - 2 * lax.rem(place, 2)
    along = place + 2 - 4 * (place // 2)
    return core, group, place, across, along, 3 - place


def greet(targets):
    barrier = pltpu.get_barrier_semaphore()
    for target in targets:
        pl.semaphore_signal(barrier, inc=1, device_id=target, device_id_type=MESH)
    pl.semaphore_wait(barrier, len(targets))


def send(source, landing, send_sem, recv_sem, target):
    return pltpu.make_async_remote_copy(
        src_ref=source,
        dst_ref=landing,
        send_sem=send_sem,
        recv_sem=recv_sem,
        device_id=target,
        device_id_type=MESH,
    )


def spread_kernel(groups, both, src, out, send_sem, recv_sem, local_sem):
    core, group, place, across, along, opposite = places_of(groups)
    half = src.shape[-1] // 2

    def device(member_group, member):
        return (core, member_group * SPLIT + member)

    def at(distance, member):
        owner = lax.rem(group + groups - distance, groups) * SPLIT + member
        return out.at[core, owner] if both else out.at[owner]

    def part(block, which):
        return block.at[:, pl.ds(which * half, half)]

    side, line = device(group, across), device(group, along)
    twin = (1 - core, group * SPLIT + place)
    far = [lax.rem(group + k, groups) for k in range(groups)]
    greet([side, line] + [device(far[k], place) for k in range(1, groups)] + ([twin] if both else []))
    started = []

    def go(source, landing, kind, distance, target):
        copy = send(source, landing, send_sem.at[kind, distance], recv_sem.at[kind, distance], target)
        copy.start()
        started.append(copy)

    def arrive(block, kind, distance, target):
        send(block, block, send_sem.at[kind, distance], recv_sem.at[kind, distance], target).wait_recv()

    def block_for(member_group):
        return src if both else src.at[member_group]

    own = block_for(group)
    local = pltpu.make_async_copy(own, at(0, place), local_sem)
    local.start()
    go(own, at(0, place), 1, 0, side)
    go(own, at(0, place), 2, 0, line)
    for k in range(1, groups):
        go(block_for(far[k]), at(0, place), 0, k, device(far[k], place))
    if both:
        go(own, at(0, place), 5, 0, twin)
    for turn in range(groups + 2):
        k = turn
        if 0 < k < groups:
            block = at(k, place)
            arrive(block, 0, k, side)
            go(block, block, 1, k, side)
            go(block, block, 2, k, line)
            if both:
                go(block, block, 5, k, twin)
        k = turn - 1
        if 0 <= k < groups:
            block = at(k, across)
            arrive(block, 1, k, side)
            go(part(block, 0), part(block, 0), 3, k, line)
            if both:
                go(block, block, 6, k, twin)
            block = at(k, along)
            arrive(block, 2, k, line)
            go(part(block, 1), part(block, 1), 4, k, side)
            if both:
                go(block, block, 7, k, twin)
        k = turn - 2
        if 0 <= k < groups:
            block = at(k, opposite)
            arrive(part(block, 0), 3, k, line)
            arrive(part(block, 1), 4, k, side)
            if both:
                go(block, block, 8, k, twin)
    if both:
        for kind, member in ((5, place), (6, across), (7, along), (8, opposite)):
            for k in range(groups):
                owner = lax.rem(group + groups - k, groups) * SPLIT + member
                arrive(out.at[1 - core, owner], kind, k, twin)
    local.wait()
    for copy in started:
        copy.wait_send()


def spread(blocks, both, identity):
    dp_count = lax.axis_size("dp")
    groups = dp_count // SPLIT
    shape = (dp_count,) + blocks.shape[-2:]
    kinds = 9 if both else 5
    return pl.pallas_call(
        lambda *refs: spread_kernel(groups, both, *refs),
        out_shape=jax.ShapeDtypeStruct(((2,) if both else ()) + shape, blocks.dtype),
        in_specs=[pl.BlockSpec(memory_space=pl.ANY)],
        out_specs=pl.BlockSpec(memory_space=pl.ANY),
        scratch_shapes=[
            pltpu.SemaphoreType.DMA((kinds, groups)),
            pltpu.SemaphoreType.DMA((kinds, groups)),
            pltpu.SemaphoreType.DMA,
        ],
        compiler_params=pltpu.CompilerParams(collective_id=identity, has_side_effects=True),
    )(blocks)


def collapse_kernel(groups, total, src, out, near, passed, pair, leaving, landed, send_sem, recv_sem):
    core, group, place, across, along, opposite = places_of(groups)
    half = src.shape[-1] // 2

    def device(member_group, member):
        return (core, member_group * SPLIT + member)

    side, line = device(group, across), device(group, along)
    far = [lax.rem(group + k, groups) for k in range(groups)]
    back = [lax.rem(group + groups - k, groups) for k in range(groups)]
    greet([side, line] + [device(far[k], place) for k in range(1, groups)])
    order = list(range(1, groups)) + [0]
    started = []

    def copy_of(source, landing, kind, k, target):
        return send(source, landing, send_sem.at[kind, k], recv_sem.at[kind, k], target)

    def go(*parts):
        copy = copy_of(*parts)
        copy.start()
        started.append(copy)

    wide = jnp.float32
    first, second = pl.ds(0, half), pl.ds(half, half)
    for k in order:
        block = src.at[far[k] * SPLIT + opposite]
        go(block.at[:, first], near.at[0, k], 0, k, line)
        go(block.at[:, second], near.at[1, k], 1, k, side)
    for k in order:
        index = far[k] * SPLIT + across
        copy_of(near.at[0, k], near.at[0, k], 0, k, line).wait_recv()
        passed[0, k, :, first] = (
            src[index, :, first].astype(wide) + near[0, k].astype(wide)
        ).astype(jnp.bfloat16)
        passed[0, k, :, second] = src[index, :, second]
        go(passed.at[0, k], pair.at[0, k], 2, k, side)
        index = far[k] * SPLIT + along
        copy_of(near.at[1, k], near.at[1, k], 1, k, side).wait_recv()
        passed[1, k, :, second] = (
            src[index, :, second].astype(wide) + near[1, k].astype(wide)
        ).astype(jnp.bfloat16)
        passed[1, k, :, first] = src[index, :, first]
        go(passed.at[1, k], pair.at[1, k], 3, k, line)
    for k in order:
        copy_of(pair.at[0, k], pair.at[0, k], 2, k, side).wait_recv()
        copy_of(pair.at[1, k], pair.at[1, k], 3, k, line).wait_recv()
        whole = (
            src[far[k] * SPLIT + place].astype(wide)
            + pair[0, k].astype(wide)
            + pair[1, k].astype(wide)
        )
        if k > 0:
            leaving[k] = whole.astype(jnp.bfloat16)
            go(leaving.at[k], landed.at[k], 4, k, device(far[k], place))
        elif total:
            out[...] = whole
        else:
            out[group] = whole.astype(jnp.bfloat16)
    for k in range(1, groups):
        copy_of(landed.at[k], landed.at[k], 4, k, side).wait_recv()
        if total:
            out[...] += landed[k].astype(wide)
        else:
            out[back[k]] = landed[k]
    for copy in started:
        copy.wait_send()


def collapse(blocks, total, identity):
    groups = blocks.shape[0] // SPLIT
    rows, columns = blocks.shape[1:]
    result = (
        jax.ShapeDtypeStruct((rows, columns), jnp.float32)
        if total
        else jax.ShapeDtypeStruct((groups, rows, columns), blocks.dtype)
    )
    vmem = pl.BlockSpec(memory_space=pltpu.VMEM)
    return pl.pallas_call(
        lambda *refs: collapse_kernel(groups, total, *refs),
        out_shape=result,
        in_specs=[vmem],
        out_specs=vmem,
        scratch_shapes=[
            pltpu.VMEM((2, groups, rows, columns // 2), blocks.dtype),
            pltpu.VMEM((2, groups, rows, columns), blocks.dtype),
            pltpu.VMEM((2, groups, rows, columns), blocks.dtype),
            pltpu.VMEM((groups, rows, columns), blocks.dtype),
            pltpu.VMEM((groups, rows, columns), blocks.dtype),
            pltpu.SemaphoreType.DMA((5, groups)),
            pltpu.SemaphoreType.DMA((5, groups)),
        ],
        compiler_params=pltpu.CompilerParams(
            collective_id=identity, has_side_effects=True, vmem_limit_bytes=36 << 20
        ),
    )(blocks)


def spread_copies(select, token_rows):
    grouped = jnp.einsum(
        "ect,td->ecd", select, token_rows, preferred_element_type=jnp.float32
    ).astype(jnp.bfloat16)
    return spread(grouped, False, 1)


def rms_back(grad_rows, inputs, scale_rows):
    normal_rows = inputs * scale_rows
    return scale_rows * (
        grad_rows - normal_rows * jnp.mean(grad_rows * normal_rows, axis=-1, keepdims=True)
    )


def smooth(values):
    return jax.nn.gelu(values, approximate=True)


def layer_forward(layer_in, weights, route_now, lengths, weight_in, weight_back):
    gain_one, w_qkv, table, w_out, gain_two, w_route = weights
    row_count, model_width = layer_in.shape
    dp_count = lax.axis_size("dp")
    expert_count = w_route.shape[1]
    slot_count = 3 * row_count * SPLIT // (2 * dp_count)
    scale_one = lax.rsqrt(jnp.mean(layer_in * layer_in, axis=-1, keepdims=True) + EPSILON)
    normed = (layer_in * scale_one * gain_one.astype(jnp.float32)).astype(jnp.bfloat16)
    qkv_rows = jnp.dot(normed, w_qkv, preferred_element_type=jnp.float32).astype(jnp.bfloat16)
    query_heads, key_heads, value_heads = split_heads(qkv_rows)
    score_bias, bucket_picks = bias_of(table, row_count)
    same_doc = same_of(lengths, row_count)
    scores = scores_of(query_heads, key_heads, score_bias, same_doc)
    row_max = jnp.max(scores, axis=-1, keepdims=True)
    exp_rows = jnp.exp(scores - row_max)
    exp_total = jnp.sum(exp_rows, axis=-1, keepdims=True)
    soft_rows = exp_rows / exp_total
    soft_low = soft_rows.astype(jnp.bfloat16)
    attended = jnp.einsum("hts,shd->thd", soft_low, value_heads, preferred_element_type=jnp.float32)
    attended = attended.reshape(row_count, model_width).astype(jnp.bfloat16)
    middle = layer_in + jnp.dot(attended, w_out, preferred_element_type=jnp.float32)
    scale_two = lax.rsqrt(jnp.mean(middle * middle, axis=-1, keepdims=True) + EPSILON)
    routed = (middle * scale_two * gain_two.astype(jnp.float32)).astype(jnp.bfloat16)
    logits = jnp.dot(routed, w_route, preferred_element_type=jnp.float32)
    choice_prob = jax.nn.softmax(logits, axis=-1)
    picked = (route_now[:, None] == jnp.arange(expert_count, dtype=jnp.int32)[None, :]).astype(
        jnp.float32
    )
    gate_prob = jnp.sum(choice_prob * picked, axis=-1)
    select = placement_of(route_now, expert_count, slot_count)
    arrived = spread_copies(select, routed)
    token_rows = arrived.reshape(-1, model_width)
    hidden = jnp.dot(token_rows, weight_in, preferred_element_type=jnp.float32)
    active = smooth(hidden).astype(jnp.bfloat16)
    partial_out = (
        jnp.dot(active, weight_back, preferred_element_type=jnp.float32)
        .astype(jnp.bfloat16)
        .reshape(arrived.shape)
    )
    returned = collapse(partial_out, False, 2)
    hidden = hidden.reshape(arrived.shape[0], arrived.shape[1], -1)
    combined = jnp.einsum(
        "ecd,ect->td",
        returned,
        select,
        preferred_element_type=jnp.float32,
    )
    result = middle + gate_prob[:, None] * combined
    kept_state = (
        layer_in,
        scale_one,
        normed,
        qkv_rows,
        soft_rows,
        attended,
        middle,
        scale_two,
        routed,
        choice_prob,
        gate_prob,
        combined,
        hidden,
        arrived,
    )
    return (result, kept_state)


def layer_backward(upstream, kept_state, weights, route_now, lengths, weight_in, weight_back):
    (
        layer_in,
        scale_one,
        normed,
        qkv_rows,
        soft_rows,
        attended,
        middle,
        scale_two,
        routed,
        choice_prob,
        gate_prob,
        combined,
        hidden,
        arrived,
    ) = kept_state
    gain_one, w_qkv, table, w_out, gain_two, w_route = weights
    row_count, model_width = layer_in.shape
    dp_count = lax.axis_size("dp")
    expert_count = w_route.shape[1]
    slot_count = 3 * row_count * SPLIT // (2 * dp_count)
    picked = (route_now[:, None] == jnp.arange(expert_count, dtype=jnp.int32)[None, :]).astype(
        jnp.float32
    )
    select = placement_of(route_now, expert_count, slot_count)
    down_grad = (gate_prob[:, None] * upstream).astype(jnp.bfloat16)
    gate_grad = jnp.sum(upstream * combined, axis=-1)
    logit_grad = (choice_prob * (picked - gate_prob[:, None]) * gate_grad[:, None]).astype(
        jnp.bfloat16
    )
    routed_grad = jnp.einsum("te,de->td", logit_grad, w_route, preferred_element_type=jnp.float32)
    arrived_grad = spread_copies(select, down_grad)
    rows_grad = arrived_grad.reshape(-1, model_width)
    active_grad = jnp.einsum(
        "rd,fd->rf", rows_grad, weight_back, preferred_element_type=jnp.float32
    )
    hidden_rows = hidden.reshape(rows_grad.shape[0], -1)
    active_rows, smooth_pull = jax.vjp(smooth, hidden_rows)
    hidden_grad = smooth_pull(active_grad)[0].astype(jnp.bfloat16)
    active_low = active_rows.astype(jnp.bfloat16)
    arrived_rows = arrived.reshape(-1, model_width)
    copy_grad = jnp.einsum(
        "rf,df->rd", hidden_grad, weight_in, preferred_element_type=jnp.float32
    ).astype(jnp.bfloat16)
    copy_back = collapse(copy_grad.reshape(dp_count, slot_count, model_width), False, 2)
    routed_grad = routed_grad + jnp.einsum(
        "ecd,ect->td",
        copy_back,
        select,
        preferred_element_type=jnp.float32,
    )
    gain_two_grad = jnp.sum(routed_grad * middle * scale_two, axis=0)
    middle_grad = upstream + rms_back(routed_grad * gain_two.astype(jnp.float32), middle, scale_two)
    branch_grad = middle_grad.astype(jnp.bfloat16)
    attended_grad = jnp.einsum(
        "te,de->td", branch_grad, w_out, preferred_element_type=jnp.float32
    ).astype(jnp.bfloat16)
    attended_grad = attended_grad.reshape(row_count, HEADS, HD)
    query_heads, key_heads, value_heads = split_heads(qkv_rows)
    bucket_picks = picks_of(row_count)
    value_grad = jnp.einsum(
        "hts,thd->shd",
        soft_rows.astype(jnp.bfloat16),
        attended_grad,
        preferred_element_type=jnp.float32,
    )
    prob_grad = jnp.einsum(
        "thd,shd->hts", attended_grad, value_heads, preferred_element_type=jnp.float32
    )
    score_grad = (
        soft_rows * (prob_grad - jnp.sum(soft_rows * prob_grad, axis=-1, keepdims=True))
    ).astype(jnp.bfloat16)
    query_grad = jnp.einsum(
        "hts,shd->thd", score_grad, key_heads, preferred_element_type=jnp.float32
    ) * (1.0 / math.sqrt(HD))
    key_grad = jnp.einsum(
        "hts,thd->shd", score_grad, query_heads, preferred_element_type=jnp.float32
    ) * (1.0 / math.sqrt(HD))
    table_grad = jnp.einsum(
        "tsb,hts->bh", bucket_picks, score_grad, preferred_element_type=jnp.float32
    ).reshape(-1)
    qkv_grad = jnp.concatenate(
        [
            query_grad.reshape(row_count, model_width),
            key_grad.reshape(row_count, model_width),
            value_grad.reshape(row_count, model_width),
        ],
        axis=1,
    ).astype(jnp.bfloat16)
    normed_grad = jnp.einsum("te,de->td", qkv_grad, w_qkv, preferred_element_type=jnp.float32)
    gain_one_grad = jnp.sum(normed_grad * layer_in * scale_one, axis=0)
    input_grad = middle_grad + rms_back(
        normed_grad * gain_one.astype(jnp.float32), layer_in, scale_one
    )
    small_grads = (gain_one_grad, table_grad, gain_two_grad)
    factor_rows = (normed, qkv_grad, attended, branch_grad, routed, logit_grad)
    expert_rows = (arrived_rows, hidden_grad, active_low, rows_grad)
    return (input_grad, small_grads, factor_rows, expert_rows)


def shared_from(small_grads, factor_rows):
    normed, qkv_grad, attended, branch_grad, routed, logit_grad = factor_rows
    qkv_weight_grad = jnp.einsum("td,te->de", normed, qkv_grad, preferred_element_type=jnp.float32)
    out_weight_grad = jnp.einsum(
        "td,te->de", attended, branch_grad, preferred_element_type=jnp.float32
    )
    route_weight_grad = jnp.einsum(
        "td,te->de", routed, logit_grad, preferred_element_type=jnp.float32
    )
    return (
        small_grads[0],
        qkv_weight_grad,
        small_grads[1],
        out_weight_grad,
        small_grads[2],
        route_weight_grad,
    )


SMALL = 256


def swap_cores(block):
    return lax.ppermute(block, "section", [(0, 1), (1, 0)])


def per_core(section_index, first_one, second_one):
    return jnp.where(section_index == 0, first_one, second_one)


def pack_columns(wide, square, columns):
    small = jnp.concatenate(columns, axis=1)
    small = jnp.pad(small, ((0, 0), (0, SMALL - small.shape[1])))
    return jnp.concatenate([wide, square, small], axis=1)


def spaced(table, group_count):
    table = table.reshape(group_count, -1)
    row_share = 2 * table.shape[1]
    return jnp.pad(table, ((0, 0), (0, row_share - table.shape[1]))).reshape(-1, 1)


def unpack_weights(packed, width, expert_count):
    dp_count = lax.axis_size("dp")
    small = packed[:, 4 * width :]
    table = small[:, 2].reshape(dp_count, -1)
    table = table[:, : table.shape[1] // 2].reshape(-1)
    return (
        small[:, 0],
        packed[:, : 3 * width],
        table,
        packed[:, 3 * width : 4 * width],
        small[:, 1],
        small[:, 3 : 3 + expert_count],
    )


def shards(
    tokens,
    out_grad,
    routes,
    doc_lengths,
    norm_attn,
    attn_qkv,
    rel_bias,
    attn_out,
    norm_ffn,
    router,
    expert_in,
    expert_out,
):
    core = lax.axis_index("section")
    dp_count = lax.axis_size("dp")
    width = tokens.shape[2]
    expert_count = router.shape[2]
    own_pack = pack_columns(
        attn_qkv[0],
        attn_out[0],
        [norm_attn[0][:, None], norm_ffn[0][:, None], spaced(rel_bias[0], 1), router[0]],
    )
    packs = spread(own_pack, True, 0)
    weights = [
        unpack_weights(packs[layer].reshape(width, own_pack.shape[1]), width, expert_count)
        for layer in range(2)
    ]
    other_in = swap_cores(expert_in[0, 0])
    other_out = swap_cores(expert_out[0, 0])
    ins = [per_core(core, expert_in[0, 0], other_in), per_core(core, other_in, expert_in[0, 0])]
    outs = [
        per_core(core, expert_out[0, 0], other_out),
        per_core(core, other_out, expert_out[0, 0]),
    ]
    route_table = routes[0, :, :, 0]
    other_route = swap_cores(per_core(core, route_table[1], route_table[0]))
    own_route = per_core(core, route_table[0], route_table[1])
    route_rows = [
        per_core(core, own_route, other_route),
        per_core(core, other_route, own_route),
    ]
    lengths = per_core(core, doc_lengths[0, 0], doc_lengths[1, 0])
    layer_in = per_core(core, tokens[0], tokens[1]).astype(jnp.float32)
    kept, lows = [], []
    for layer in range(2):
        result, state = layer_forward(
            layer_in, weights[layer], route_rows[layer], lengths, ins[layer], outs[layer]
        )
        low = result.astype(jnp.bfloat16)
        lows.append(low)
        kept.append(state)
        layer_in = low.astype(jnp.float32)

    def sorted_out(pair):
        mine = per_core(core, pair[0], pair[1])
        theirs = swap_cores(per_core(core, pair[1], pair[0]))
        return jnp.stack([per_core(core, mine, theirs), per_core(core, theirs, mine)])

    upstream = per_core(core, out_grad[0], out_grad[1]).astype(jnp.float32)
    input_grads, expert_rows = [None, None], [None, None]
    factors, smalls = [None, None], [None, None]
    for layer in (1, 0):
        input_grad, smalls[layer], factors[layer], expert_rows[layer] = layer_backward(
            upstream,
            kept[layer],
            weights[layer],
            route_rows[layer],
            lengths,
            ins[layer],
            outs[layer],
        )
        input_grads[layer] = input_grad
        upstream = input_grad.astype(jnp.bfloat16).astype(jnp.float32)

    def own_layer(pair):
        mine = per_core(core, pair[0], pair[1])
        return mine, swap_cores(per_core(core, pair[1], pair[0]))

    joined = own_layer([jnp.concatenate(group, axis=1) for group in factors])
    joined = jnp.concatenate(joined, axis=0)
    ends = np.cumsum([member.shape[1] for member in factors[0]])
    factor_rows = [
        joined[:, end - member.shape[1] : end] for end, member in zip(ends, factors[0])
    ]
    small_pair = own_layer([jnp.concatenate(group, axis=0) for group in smalls])
    small_sum = small_pair[0] + small_pair[1]
    small_grads = (
        small_sum[:width],
        small_sum[width:-width],
        small_sum[-width:],
    )
    totals = shared_from(small_grads, factor_rows)
    packed = pack_columns(
        totals[1],
        totals[3],
        [totals[0][:, None], totals[4][:, None], spaced(totals[2], dp_count), totals[5]],
    ).astype(jnp.bfloat16)
    total = collapse(packed.reshape(dp_count, -1, packed.shape[1]), True, 3)

    def joined_rows(index):
        mine = per_core(core, expert_rows[0][index], expert_rows[1][index])
        theirs = swap_cores(per_core(core, expert_rows[1][index], expert_rows[0][index]))
        return jnp.concatenate([mine, theirs], axis=0)

    arrived_all, hidden_grad_all, active_all, rows_grad_all = [joined_rows(i) for i in range(4)]
    in_total = jnp.einsum(
        "rd,rf->df", arrived_all, hidden_grad_all, preferred_element_type=jnp.float32
    )
    back_total = jnp.einsum(
        "rf,rd->fd", active_all, rows_grad_all, preferred_element_type=jnp.float32
    )
    outputs = sorted_out(lows)
    input_store = sorted_out(input_grads)
    small = total[:, 4 * width :]
    return (
        outputs[None],
        input_store[None],
        small[None, :, 0],
        total[None, :, : 3 * width],
        small[None, : rel_bias.shape[1], 2],
        total[None, :, 3 * width : 4 * width],
        small[None, :, 1],
        small[None, :, 3 : 3 + expert_count],
        in_total[None, None],
        back_total[None, None],
    )


def solution(mesh):
    placed = (
        P(None, "dp", None),
        P(None, "dp", None),
        P("section", None, "dp", None),
        P(None, "dp", None),
        P("section", "dp"),
        P("section", "dp", None),
        P("section", "dp"),
        P("section", "dp", None),
        P("section", "dp"),
        P("section", "dp", None),
        P("section", "dp", None, None),
        P("section", "dp", None, None),
    )
    return jax.shard_map(
        shards,
        mesh=mesh,
        in_specs=placed,
        out_specs=(
            P("section", None, "dp", None),
            P("section", None, "dp", None),
            P("section", "dp"),
            P("section", "dp", None),
            P("section", "dp"),
            P("section", "dp", None),
            P("section", "dp"),
            P("section", "dp", None),
            P("section", "dp", None, None),
            P("section", "dp", None, None),
        ),
        check_vma=False,
    )
```

```python
import math

import jax
import jax.numpy as jnp
import numpy as np
from jax import lax
from jax.experimental import pallas as pl
from jax.experimental.pallas import tpu as pltpu
from jax.sharding import PartitionSpec as P

HEADS = 12
HD = 64
BUCKETS = 32
SPLIT = 4


EPSILON = 1e-06
far_limits = np.array([8, 12, 16, 23, 32, 46, 64, 91], dtype=np.int32)


def buckets_of(row_count):
    places = jnp.arange(row_count, dtype=jnp.int32)
    offset = places[None, :] - places[:, None]
    distance = jnp.abs(offset)
    beyond = jnp.sum(
        (distance[:, :, None] >= jnp.asarray(far_limits)[None, None, :]).astype(jnp.int32), axis=-1
    )
    nearby = jnp.where(distance < 8, distance, 7 + beyond)
    upward = jnp.where(offset > 0, BUCKETS // 2, 0).astype(jnp.int32)
    return nearby + upward


def documents_of(lengths, row_count):
    ending = jnp.cumsum(lengths, axis=-1)
    places = jnp.arange(row_count, dtype=jnp.int32)
    return jnp.sum((places[:, None] >= ending[..., None, :]).astype(jnp.int32), axis=-1)


def same_of(lengths, row_count):
    documents = documents_of(lengths, row_count)
    return documents[:, None] == documents[None, :]


def picks_of(row_count):
    return (
        buckets_of(row_count)[:, :, None] == jnp.arange(BUCKETS, dtype=jnp.int32)[None, None, :]
    ).astype(jnp.bfloat16)


def bias_of(table, row_count):
    bucket_picks = picks_of(row_count)
    score_bias = jnp.einsum(
        "tsb,bh->hts",
        bucket_picks,
        table.reshape(BUCKETS, HEADS),
        preferred_element_type=jnp.float32,
    )
    return (score_bias, bucket_picks)


def split_heads(qkv_rows):
    row_count = qkv_rows.shape[0]
    model_width = qkv_rows.shape[1] // 3
    query_heads = qkv_rows[:, :model_width].reshape(row_count, HEADS, HD)
    key_heads = qkv_rows[:, model_width : 2 * model_width].reshape(row_count, HEADS, HD)
    value_heads = qkv_rows[:, 2 * model_width :].reshape(row_count, HEADS, HD)
    return (query_heads, key_heads, value_heads)


def scores_of(query_heads, key_heads, score_bias, same_doc):
    raw_scores = (
        jnp.einsum("thd,shd->hts", query_heads, key_heads, preferred_element_type=jnp.float32)
        * (1.0 / math.sqrt(HD))
        + score_bias
    )
    return jnp.where(same_doc[None], raw_scores, -1000000000.0)


def placement_of(route_now, expert_count, slot_count):
    row_count = route_now.shape[0]
    places = jnp.arange(row_count, dtype=jnp.int32)
    earlier = (route_now[:, None] == route_now[None, :]) & (places[None, :] < places[:, None])
    ranks = jnp.sum(earlier.astype(jnp.int32), axis=1)
    target = route_now * slot_count + ranks
    flat = (
        jnp.arange(expert_count * slot_count, dtype=jnp.int32)[:, None] == target[None, :]
    ).astype(jnp.bfloat16)
    return flat.reshape(expert_count, slot_count, row_count)


MESH = pl.DeviceIdType.MESH


def places_of(groups):
    core = lax.axis_index("section")
    me = lax.axis_index("dp")
    group, place = me // SPLIT, lax.rem(me, SPLIT)
    across = place + 1 - 2 * lax.rem(place, 2)
    along = place + 2 - 4 * (place // 2)
    return core, group, place, across, along, 3 - place


def greet(targets):
    barrier = pltpu.get_barrier_semaphore()
    for target in targets:
        pl.semaphore_signal(barrier, inc=1, device_id=target, device_id_type=MESH)
    pl.semaphore_wait(barrier, len(targets))


def send(source, landing, send_sem, recv_sem, target):
    return pltpu.make_async_remote_copy(
        src_ref=source,
        dst_ref=landing,
        send_sem=send_sem,
        recv_sem=recv_sem,
        device_id=target,
        device_id_type=MESH,
    )


def spread_kernel(groups, both, src, out, send_sem, recv_sem, local_sem):
    core, group, place, across, along, opposite = places_of(groups)
    half = src.shape[-1] // 2

    def device(member_group, member):
        return (core, member_group * SPLIT + member)

    def at(distance, member):
        owner = lax.rem(group + groups - distance, groups) * SPLIT + member
        return out.at[core, owner] if both else out.at[owner]

    def part(block, which):
        return block.at[:, pl.ds(which * half, half)]

    side, line = device(group, across), device(group, along)
    twin = (1 - core, group * SPLIT + place)
    far = [lax.rem(group + k, groups) for k in range(groups)]
    greet([side, line] + [device(far[k], place) for k in range(1, groups)] + ([twin] if both else []))
    started = []

    def go(source, landing, kind, distance, target):
        copy = send(source, landing, send_sem.at[kind, distance], recv_sem.at[kind, distance], target)
        copy.start()
        started.append(copy)

    def arrive(block, kind, distance, target):
        send(block, block, send_sem.at[kind, distance], recv_sem.at[kind, distance], target).wait_recv()

    def block_for(member_group):
        return src if both else src.at[member_group]

    own = block_for(group)
    local = pltpu.make_async_copy(own, at(0, place), local_sem)
    local.start()
    go(own, at(0, place), 1, 0, side)
    go(own, at(0, place), 2, 0, line)
    for k in range(1, groups):
        go(block_for(far[k]), at(0, place), 0, k, device(far[k], place))
    if both:
        go(own, at(0, place), 5, 0, twin)
    for turn in range(groups + 2):
        k = turn
        if 0 < k < groups:
            block = at(k, place)
            arrive(block, 0, k, side)
            go(block, block, 1, k, side)
            go(block, block, 2, k, line)
            if both:
                go(block, block, 5, k, twin)
        k = turn - 1
        if 0 <= k < groups:
            block = at(k, across)
            arrive(block, 1, k, side)
            go(part(block, 0), part(block, 0), 3, k, line)
            if both:
                go(block, block, 6, k, twin)
            block = at(k, along)
            arrive(block, 2, k, line)
            go(part(block, 1), part(block, 1), 4, k, side)
            if both:
                go(block, block, 7, k, twin)
        k = turn - 2
        if 0 <= k < groups:
            block = at(k, opposite)
            arrive(part(block, 0), 3, k, line)
            arrive(part(block, 1), 4, k, side)
            if both:
                go(block, block, 8, k, twin)
    if both:
        for kind, member in ((5, place), (6, across), (7, along), (8, opposite)):
            for k in range(groups):
                owner = lax.rem(group + groups - k, groups) * SPLIT + member
                arrive(out.at[1 - core, owner], kind, k, twin)
    local.wait()
    for copy in started:
        copy.wait_send()


def spread(blocks, both, identity):
    dp_count = lax.axis_size("dp")
    groups = dp_count // SPLIT
    shape = (dp_count,) + blocks.shape[-2:]
    kinds = 9 if both else 5
    space = pl.BlockSpec(memory_space=pl.ANY if both else pltpu.VMEM)
    return pl.pallas_call(
        lambda *refs: spread_kernel(groups, both, *refs),
        out_shape=jax.ShapeDtypeStruct(((2,) if both else ()) + shape, blocks.dtype),
        in_specs=[space],
        out_specs=space,
        scratch_shapes=[
            pltpu.SemaphoreType.DMA((kinds, groups)),
            pltpu.SemaphoreType.DMA((kinds, groups)),
            pltpu.SemaphoreType.DMA,
        ],
        compiler_params=pltpu.CompilerParams(collective_id=identity, has_side_effects=True),
    )(blocks)


def collapse_kernel(groups, total, src, out, near, passed, pair, leaving, landed, send_sem, recv_sem):
    core, group, place, across, along, opposite = places_of(groups)
    half = src.shape[-1] // 2

    def device(member_group, member):
        return (core, member_group * SPLIT + member)

    side, line = device(group, across), device(group, along)
    far = [lax.rem(group + k, groups) for k in range(groups)]
    back = [lax.rem(group + groups - k, groups) for k in range(groups)]
    greet([side, line] + [device(far[k], place) for k in range(1, groups)])
    order = list(range(1, groups)) + [0]
    started = []

    def copy_of(source, landing, kind, k, target):
        return send(source, landing, send_sem.at[kind, k], recv_sem.at[kind, k], target)

    def go(*parts):
        copy = copy_of(*parts)
        copy.start()
        started.append(copy)

    wide = jnp.float32
    first, second = pl.ds(0, half), pl.ds(half, half)
    for k in order:
        block = src.at[far[k] * SPLIT + opposite]
        go(block.at[:, first], near.at[0, k], 0, k, line)
        go(block.at[:, second], near.at[1, k], 1, k, side)
    for k in order:
        index = far[k] * SPLIT + across
        copy_of(near.at[0, k], near.at[0, k], 0, k, line).wait_recv()
        passed[0, k, :, first] = (
            src[index, :, first].astype(wide) + near[0, k].astype(wide)
        ).astype(jnp.bfloat16)
        passed[0, k, :, second] = src[index, :, second]
        go(passed.at[0, k], pair.at[0, k], 2, k, side)
        index = far[k] * SPLIT + along
        copy_of(near.at[1, k], near.at[1, k], 1, k, side).wait_recv()
        passed[1, k, :, second] = (
            src[index, :, second].astype(wide) + near[1, k].astype(wide)
        ).astype(jnp.bfloat16)
        passed[1, k, :, first] = src[index, :, first]
        go(passed.at[1, k], pair.at[1, k], 3, k, line)
    for k in order:
        copy_of(pair.at[0, k], pair.at[0, k], 2, k, side).wait_recv()
        copy_of(pair.at[1, k], pair.at[1, k], 3, k, line).wait_recv()
        whole = (
            src[far[k] * SPLIT + place].astype(wide)
            + pair[0, k].astype(wide)
            + pair[1, k].astype(wide)
        )
        if k > 0:
            leaving[k] = whole.astype(jnp.bfloat16)
            go(leaving.at[k], landed.at[k], 4, k, device(far[k], place))
        elif total:
            out[...] = whole
        else:
            out[group] = whole.astype(jnp.bfloat16)
    for k in range(1, groups):
        copy_of(landed.at[k], landed.at[k], 4, k, side).wait_recv()
        if total:
            out[...] += landed[k].astype(wide)
        else:
            out[back[k]] = landed[k]
    for copy in started:
        copy.wait_send()


def collapse(blocks, total, identity):
    groups = blocks.shape[0] // SPLIT
    rows, columns = blocks.shape[1:]
    result = (
        jax.ShapeDtypeStruct((rows, columns), jnp.float32)
        if total
        else jax.ShapeDtypeStruct((groups, rows, columns), blocks.dtype)
    )
    vmem = pl.BlockSpec(memory_space=pltpu.VMEM)
    return pl.pallas_call(
        lambda *refs: collapse_kernel(groups, total, *refs),
        out_shape=result,
        in_specs=[vmem],
        out_specs=vmem,
        scratch_shapes=[
            pltpu.VMEM((2, groups, rows, columns // 2), blocks.dtype),
            pltpu.VMEM((2, groups, rows, columns), blocks.dtype),
            pltpu.VMEM((2, groups, rows, columns), blocks.dtype),
            pltpu.VMEM((groups, rows, columns), blocks.dtype),
            pltpu.VMEM((groups, rows, columns), blocks.dtype),
            pltpu.SemaphoreType.DMA((5, groups)),
            pltpu.SemaphoreType.DMA((5, groups)),
        ],
        compiler_params=pltpu.CompilerParams(
            collective_id=identity, has_side_effects=True, vmem_limit_bytes=36 << 20
        ),
    )(blocks)


def grouped_rows(select, token_rows):
    return jnp.einsum(
        "ect,td->ecd", select, token_rows, preferred_element_type=jnp.float32
    ).astype(jnp.bfloat16)


def rms_back(grad_rows, inputs, scale_rows):
    normal_rows = inputs * scale_rows
    return scale_rows * (
        grad_rows - normal_rows * jnp.mean(grad_rows * normal_rows, axis=-1, keepdims=True)
    )


def smooth(values):
    return jax.nn.gelu(values, approximate=True)


def expert_pull(hidden_rows, rows_grad, weight_in, weight_back):
    active_grad = jnp.einsum(
        "rd,fd->rf", rows_grad, weight_back, preferred_element_type=jnp.float32
    )
    smooth_pull = jax.vjp(smooth, hidden_rows)[1]
    hidden_grad = smooth_pull(active_grad)[0].astype(jnp.bfloat16)
    copy_grad = jnp.einsum(
        "rf,df->rd", hidden_grad, weight_in, preferred_element_type=jnp.float32
    ).astype(jnp.bfloat16)
    return hidden_grad, copy_grad


def layer_forward(layer_in, weights, route_now, lengths, weight_in, weight_back, upstream=None):
    gain_one, w_qkv, table, w_out, gain_two, w_route = weights
    row_count, model_width = layer_in.shape
    dp_count = lax.axis_size("dp")
    expert_count = w_route.shape[1]
    slot_count = 3 * row_count * SPLIT // (2 * dp_count)
    scale_one = lax.rsqrt(jnp.mean(layer_in * layer_in, axis=-1, keepdims=True) + EPSILON)
    normed = (layer_in * scale_one * gain_one.astype(jnp.float32)).astype(jnp.bfloat16)
    qkv_rows = jnp.dot(normed, w_qkv, preferred_element_type=jnp.float32).astype(jnp.bfloat16)
    query_heads, key_heads, value_heads = split_heads(qkv_rows)
    score_bias, bucket_picks = bias_of(table, row_count)
    same_doc = same_of(lengths, row_count)
    scores = scores_of(query_heads, key_heads, score_bias, same_doc)
    row_max = jnp.max(scores, axis=-1, keepdims=True)
    exp_rows = jnp.exp(scores - row_max)
    exp_total = jnp.sum(exp_rows, axis=-1, keepdims=True)
    soft_rows = exp_rows / exp_total
    soft_low = soft_rows.astype(jnp.bfloat16)
    attended = jnp.einsum("hts,shd->thd", soft_low, value_heads, preferred_element_type=jnp.float32)
    attended = attended.reshape(row_count, model_width).astype(jnp.bfloat16)
    middle = layer_in + jnp.dot(attended, w_out, preferred_element_type=jnp.float32)
    scale_two = lax.rsqrt(jnp.mean(middle * middle, axis=-1, keepdims=True) + EPSILON)
    routed = (middle * scale_two * gain_two.astype(jnp.float32)).astype(jnp.bfloat16)
    logits = jnp.dot(routed, w_route, preferred_element_type=jnp.float32)
    choice_prob = jax.nn.softmax(logits, axis=-1)
    picked = (route_now[:, None] == jnp.arange(expert_count, dtype=jnp.int32)[None, :]).astype(
        jnp.float32
    )
    gate_prob = jnp.sum(choice_prob * picked, axis=-1)
    select = placement_of(route_now, expert_count, slot_count)
    grouped = grouped_rows(select, routed)
    if upstream is None:
        arrived = spread(grouped, False, 1)
    else:
        down_grad = (gate_prob[:, None] * upstream).astype(jnp.bfloat16)
        grouped = jnp.concatenate([grouped, grouped_rows(select, down_grad)], axis=1)
        arrived_both = spread(grouped, False, 4)
        arrived = arrived_both[:, :slot_count]
        rows_grad = arrived_both[:, slot_count:].reshape(-1, model_width)
    token_rows = arrived.reshape(-1, model_width)
    hidden = jnp.dot(token_rows, weight_in, preferred_element_type=jnp.float32)
    active = smooth(hidden).astype(jnp.bfloat16)
    partial_out = (
        jnp.dot(active, weight_back, preferred_element_type=jnp.float32)
        .astype(jnp.bfloat16)
        .reshape(arrived.shape)
    )
    if upstream is None:
        returned = collapse(partial_out, False, 2)
        early = None
    else:
        hidden_grad, copy_grad = expert_pull(hidden, rows_grad, weight_in, weight_back)
        leaving = jnp.concatenate([partial_out, copy_grad.reshape(arrived.shape)], axis=1)
        coming = collapse(leaving, False, 5)
        returned = coming[:, :slot_count]
        early = (rows_grad, hidden_grad, coming[:, slot_count:])
    hidden = hidden.reshape(arrived.shape[0], arrived.shape[1], -1)
    combined = jnp.einsum(
        "ecd,ect->td",
        returned,
        select,
        preferred_element_type=jnp.float32,
    )
    result = middle + gate_prob[:, None] * combined
    kept_state = (
        layer_in,
        scale_one,
        normed,
        qkv_rows,
        soft_rows,
        attended,
        middle,
        scale_two,
        routed,
        choice_prob,
        gate_prob,
        combined,
        active,
        hidden,
        arrived,
        early,
    )
    return (result, kept_state)


def layer_backward(upstream, kept_state, weights, route_now, lengths, weight_in, weight_back):
    (
        layer_in,
        scale_one,
        normed,
        qkv_rows,
        soft_rows,
        attended,
        middle,
        scale_two,
        routed,
        choice_prob,
        gate_prob,
        combined,
        active,
        hidden,
        arrived,
        early,
    ) = kept_state
    gain_one, w_qkv, table, w_out, gain_two, w_route = weights
    row_count, model_width = layer_in.shape
    dp_count = lax.axis_size("dp")
    expert_count = w_route.shape[1]
    slot_count = 3 * row_count * SPLIT // (2 * dp_count)
    picked = (route_now[:, None] == jnp.arange(expert_count, dtype=jnp.int32)[None, :]).astype(
        jnp.float32
    )
    select = placement_of(route_now, expert_count, slot_count)
    gate_grad = jnp.sum(upstream * combined, axis=-1)
    logit_grad = (choice_prob * (picked - gate_prob[:, None]) * gate_grad[:, None]).astype(
        jnp.bfloat16
    )
    routed_grad = jnp.einsum("te,de->td", logit_grad, w_route, preferred_element_type=jnp.float32)
    if early is None:
        down_grad = (gate_prob[:, None] * upstream).astype(jnp.bfloat16)
        rows_grad = spread(grouped_rows(select, down_grad), False, 1).reshape(-1, model_width)
        hidden_rows = hidden.reshape(rows_grad.shape[0], -1)
        hidden_grad, copy_grad = expert_pull(hidden_rows, rows_grad, weight_in, weight_back)
        copy_back = collapse(copy_grad.reshape(dp_count, slot_count, model_width), False, 2)
    else:
        rows_grad, hidden_grad, copy_back = early
    arrived_rows = arrived.reshape(-1, model_width)
    routed_grad = routed_grad + jnp.einsum(
        "ecd,ect->td",
        copy_back,
        select,
        preferred_element_type=jnp.float32,
    )
    gain_two_grad = jnp.sum(routed_grad * middle * scale_two, axis=0)
    middle_grad = upstream + rms_back(routed_grad * gain_two.astype(jnp.float32), middle, scale_two)
    branch_grad = middle_grad.astype(jnp.bfloat16)
    attended_grad = jnp.einsum(
        "te,de->td", branch_grad, w_out, preferred_element_type=jnp.float32
    ).astype(jnp.bfloat16)
    attended_grad = attended_grad.reshape(row_count, HEADS, HD)
    query_heads, key_heads, value_heads = split_heads(qkv_rows)
    bucket_picks = picks_of(row_count)
    value_grad = jnp.einsum(
        "hts,thd->shd",
        soft_rows.astype(jnp.bfloat16),
        attended_grad,
        preferred_element_type=jnp.float32,
    )
    prob_grad = jnp.einsum(
        "thd,shd->hts", attended_grad, value_heads, preferred_element_type=jnp.float32
    )
    score_grad = (
        soft_rows * (prob_grad - jnp.sum(soft_rows * prob_grad, axis=-1, keepdims=True))
    ).astype(jnp.bfloat16)
    query_grad = jnp.einsum(
        "hts,shd->thd", score_grad, key_heads, preferred_element_type=jnp.float32
    ) * (1.0 / math.sqrt(HD))
    key_grad = jnp.einsum(
        "hts,thd->shd", score_grad, query_heads, preferred_element_type=jnp.float32
    ) * (1.0 / math.sqrt(HD))
    table_grad = jnp.einsum(
        "tsb,hts->bh", bucket_picks, score_grad, preferred_element_type=jnp.float32
    ).reshape(-1)
    qkv_grad = jnp.concatenate(
        [
            query_grad.reshape(row_count, model_width),
            key_grad.reshape(row_count, model_width),
            value_grad.reshape(row_count, model_width),
        ],
        axis=1,
    ).astype(jnp.bfloat16)
    normed_grad = jnp.einsum("te,de->td", qkv_grad, w_qkv, preferred_element_type=jnp.float32)
    gain_one_grad = jnp.sum(normed_grad * layer_in * scale_one, axis=0)
    input_grad = middle_grad + rms_back(
        normed_grad * gain_one.astype(jnp.float32), layer_in, scale_one
    )
    small_grads = (gain_one_grad, table_grad, gain_two_grad)
    factor_rows = (normed, qkv_grad, attended, branch_grad, routed, logit_grad)
    expert_rows = (arrived_rows, hidden_grad, active, rows_grad)
    return (input_grad, small_grads, factor_rows, expert_rows)


def shared_from(small_grads, factor_rows):
    normed, qkv_grad, attended, branch_grad, routed, logit_grad = factor_rows
    qkv_weight_grad = jnp.einsum("td,te->de", normed, qkv_grad, preferred_element_type=jnp.float32)
    out_weight_grad = jnp.einsum(
        "td,te->de", attended, branch_grad, preferred_element_type=jnp.float32
    )
    route_weight_grad = jnp.einsum(
        "td,te->de", routed, logit_grad, preferred_element_type=jnp.float32
    )
    return (
        small_grads[0],
        qkv_weight_grad,
        small_grads[1],
        out_weight_grad,
        small_grads[2],
        route_weight_grad,
    )


SMALL = 256


def swap_cores(block):
    return lax.ppermute(block, "section", [(0, 1), (1, 0)])


def per_core(section_index, first_one, second_one):
    return jnp.where(section_index == 0, first_one, second_one)


def pack_columns(wide, square, columns):
    small = jnp.concatenate(columns, axis=1)
    small = jnp.pad(small, ((0, 0), (0, SMALL - small.shape[1])))
    return jnp.concatenate([wide, square, small], axis=1)


def spaced(table, group_count):
    table = table.reshape(group_count, -1)
    row_share = 2 * table.shape[1]
    return jnp.pad(table, ((0, 0), (0, row_share - table.shape[1]))).reshape(-1, 1)


def unpack_weights(packed, width, expert_count):
    dp_count = lax.axis_size("dp")
    small = packed[:, 4 * width :]
    table = small[:, 2].reshape(dp_count, -1)
    table = table[:, : table.shape[1] // 2].reshape(-1)
    return (
        small[:, 0],
        packed[:, : 3 * width],
        table,
        packed[:, 3 * width : 4 * width],
        small[:, 1],
        small[:, 3 : 3 + expert_count],
    )


def shards(
    tokens,
    out_grad,
    routes,
    doc_lengths,
    norm_attn,
    attn_qkv,
    rel_bias,
    attn_out,
    norm_ffn,
    router,
    expert_in,
    expert_out,
):
    core = lax.axis_index("section")
    dp_count = lax.axis_size("dp")
    width = tokens.shape[2]
    expert_count = router.shape[2]
    own_pack = pack_columns(
        attn_qkv[0],
        attn_out[0],
        [norm_attn[0][:, None], norm_ffn[0][:, None], spaced(rel_bias[0], 1), router[0]],
    )
    packs = spread(own_pack, True, 0)
    weights = [
        unpack_weights(packs[layer].reshape(width, own_pack.shape[1]), width, expert_count)
        for layer in range(2)
    ]
    other_in = swap_cores(expert_in[0, 0])
    other_out = swap_cores(expert_out[0, 0])
    ins = [per_core(core, expert_in[0, 0], other_in), per_core(core, other_in, expert_in[0, 0])]
    outs = [
        per_core(core, expert_out[0, 0], other_out),
        per_core(core, other_out, expert_out[0, 0]),
    ]
    route_table = routes[0, :, :, 0]
    other_route = swap_cores(per_core(core, route_table[1], route_table[0]))
    own_route = per_core(core, route_table[0], route_table[1])
    route_rows = [
        per_core(core, own_route, other_route),
        per_core(core, other_route, own_route),
    ]
    lengths = per_core(core, doc_lengths[0, 0], doc_lengths[1, 0])
    layer_in = per_core(core, tokens[0], tokens[1]).astype(jnp.float32)
    upstream = per_core(core, out_grad[0], out_grad[1]).astype(jnp.float32)
    kept, lows = [], []
    for layer in range(2):
        result, state = layer_forward(
            layer_in,
            weights[layer],
            route_rows[layer],
            lengths,
            ins[layer],
            outs[layer],
            upstream if layer == 1 else None,
        )
        low = result.astype(jnp.bfloat16)
        lows.append(low)
        kept.append(state)
        layer_in = low.astype(jnp.float32)

    def sorted_out(pair):
        mine = per_core(core, pair[0], pair[1])
        theirs = swap_cores(per_core(core, pair[1], pair[0]))
        return jnp.stack([per_core(core, mine, theirs), per_core(core, theirs, mine)])

    input_grads, expert_rows = [None, None], [None, None]
    factors, smalls = [None, None], [None, None]
    for layer in (1, 0):
        input_grad, smalls[layer], factors[layer], expert_rows[layer] = layer_backward(
            upstream,
            kept[layer],
            weights[layer],
            route_rows[layer],
            lengths,
            ins[layer],
            outs[layer],
        )
        input_grads[layer] = input_grad
        upstream = input_grad.astype(jnp.bfloat16).astype(jnp.float32)

    def own_layer(pair):
        mine = per_core(core, pair[0], pair[1])
        return mine, swap_cores(per_core(core, pair[1], pair[0]))

    joined = own_layer([jnp.concatenate(group, axis=1) for group in factors])
    joined = jnp.concatenate(joined, axis=0)
    ends = np.cumsum([member.shape[1] for member in factors[0]])
    factor_rows = [
        joined[:, end - member.shape[1] : end] for end, member in zip(ends, factors[0])
    ]
    small_pair = own_layer([jnp.concatenate(group, axis=0) for group in smalls])
    small_sum = small_pair[0] + small_pair[1]
    small_grads = (
        small_sum[:width],
        small_sum[width:-width],
        small_sum[-width:],
    )
    totals = shared_from(small_grads, factor_rows)
    packed = pack_columns(
        totals[1],
        totals[3],
        [totals[0][:, None], totals[4][:, None], spaced(totals[2], dp_count), totals[5]],
    ).astype(jnp.bfloat16)
    total = collapse(packed.reshape(dp_count, -1, packed.shape[1]), True, 3)

    def joined_rows(index):
        first_one, second_one = expert_rows[0][index], expert_rows[1][index]
        to_first = lax.ppermute(first_one, "section", [(1, 0)])
        to_second = lax.ppermute(second_one, "section", [(0, 1)])
        mine = per_core(core, first_one, second_one)
        theirs = per_core(core, to_first, to_second)
        return jnp.concatenate([mine, theirs], axis=0)

    arrived_all, hidden_grad_all, active_all, rows_grad_all = [joined_rows(i) for i in range(4)]
    in_total = jnp.einsum(
        "rd,rf->df", arrived_all, hidden_grad_all, preferred_element_type=jnp.float32
    )
    back_total = jnp.einsum(
        "rf,rd->fd", active_all, rows_grad_all, preferred_element_type=jnp.float32
    )
    outputs = sorted_out(lows)
    input_store = sorted_out(input_grads)
    small = total[:, 4 * width :]
    return (
        outputs[None],
        input_store[None],
        small[None, :, 0],
        total[None, :, : 3 * width],
        small[None, : rel_bias.shape[1], 2],
        total[None, :, 3 * width : 4 * width],
        small[None, :, 1],
        small[None, :, 3 : 3 + expert_count],
        in_total[None, None],
        back_total[None, None],
    )


def solution(mesh):
    placed = (
        P(None, "dp", None),
        P(None, "dp", None),
        P("section", None, "dp", None),
        P(None, "dp", None),
        P("section", "dp"),
        P("section", "dp", None),
        P("section", "dp"),
        P("section", "dp", None),
        P("section", "dp"),
        P("section", "dp", None),
        P("section", "dp", None, None),
        P("section", "dp", None, None),
    )
    return jax.shard_map(
        shards,
        mesh=mesh,
        in_specs=placed,
        out_specs=(
            P("section", None, "dp", None),
            P("section", None, "dp", None),
            P("section", "dp"),
            P("section", "dp", None),
            P("section", "dp"),
            P("section", "dp", None),
            P("section", "dp"),
            P("section", "dp", None),
            P("section", "dp", None, None),
            P("section", "dp", None, None),
        ),
        check_vma=False,
    )
```

```python
import math

import jax
import jax.numpy as jnp
import numpy as np
from jax import lax
from jax.experimental import pallas as pl
from jax.experimental.pallas import tpu as pltpu
from jax.sharding import PartitionSpec as P

HEADS = 12
HD = 64
BUCKETS = 32
SPLIT = 4


EPSILON = 1e-06
far_limits = np.array([8, 12, 16, 23, 32, 46, 64, 91], dtype=np.int32)


def buckets_of(row_count):
    places = jnp.arange(row_count, dtype=jnp.int32)
    offset = places[None, :] - places[:, None]
    distance = jnp.abs(offset)
    beyond = jnp.sum(
        (distance[:, :, None] >= jnp.asarray(far_limits)[None, None, :]).astype(jnp.int32), axis=-1
    )
    nearby = jnp.where(distance < 8, distance, 7 + beyond)
    upward = jnp.where(offset > 0, BUCKETS // 2, 0).astype(jnp.int32)
    return nearby + upward


def documents_of(lengths, row_count):
    ending = jnp.cumsum(lengths, axis=-1)
    places = jnp.arange(row_count, dtype=jnp.int32)
    return jnp.sum((places[:, None] >= ending[..., None, :]).astype(jnp.int32), axis=-1)


def same_of(lengths, row_count):
    documents = documents_of(lengths, row_count)
    return documents[:, None] == documents[None, :]


def picks_of(row_count):
    return (
        buckets_of(row_count)[:, :, None] == jnp.arange(BUCKETS, dtype=jnp.int32)[None, None, :]
    ).astype(jnp.bfloat16)


def bias_of(table, row_count):
    bucket_picks = picks_of(row_count)
    score_bias = jnp.einsum(
        "tsb,bh->hts",
        bucket_picks,
        table.reshape(BUCKETS, HEADS),
        preferred_element_type=jnp.float32,
    )
    return (score_bias, bucket_picks)


def split_heads(qkv_rows):
    row_count = qkv_rows.shape[0]
    model_width = qkv_rows.shape[1] // 3
    query_heads = qkv_rows[:, :model_width].reshape(row_count, HEADS, HD)
    key_heads = qkv_rows[:, model_width : 2 * model_width].reshape(row_count, HEADS, HD)
    value_heads = qkv_rows[:, 2 * model_width :].reshape(row_count, HEADS, HD)
    return (query_heads, key_heads, value_heads)


def scores_of(query_heads, key_heads, score_bias, same_doc):
    raw_scores = (
        jnp.einsum("thd,shd->hts", query_heads, key_heads, preferred_element_type=jnp.float32)
        * (1.0 / math.sqrt(HD))
        + score_bias
    )
    return jnp.where(same_doc[None], raw_scores, -1000000000.0)


def placement_of(route_now, expert_count, slot_count):
    row_count = route_now.shape[0]
    places = jnp.arange(row_count, dtype=jnp.int32)
    earlier = (route_now[:, None] == route_now[None, :]) & (places[None, :] < places[:, None])
    ranks = jnp.sum(earlier.astype(jnp.int32), axis=1)
    target = route_now * slot_count + ranks
    flat = (
        jnp.arange(expert_count * slot_count, dtype=jnp.int32)[:, None] == target[None, :]
    ).astype(jnp.bfloat16)
    return flat.reshape(expert_count, slot_count, row_count)


MESH = pl.DeviceIdType.MESH


def places_of(groups):
    core = lax.axis_index("section")
    me = lax.axis_index("dp")
    group, place = me // SPLIT, lax.rem(me, SPLIT)
    across = place + 1 - 2 * lax.rem(place, 2)
    along = place + 2 - 4 * (place // 2)
    return core, group, place, across, along, 3 - place


def greet(targets):
    barrier = pltpu.get_barrier_semaphore()
    for target in targets:
        pl.semaphore_signal(barrier, inc=1, device_id=target, device_id_type=MESH)
    pl.semaphore_wait(barrier, len(targets))


def send(source, landing, send_sem, recv_sem, target):
    return pltpu.make_async_remote_copy(
        src_ref=source,
        dst_ref=landing,
        send_sem=send_sem,
        recv_sem=recv_sem,
        device_id=target,
        device_id_type=MESH,
    )


def spread_kernel(groups, both, src, out, send_sem, recv_sem, local_sem):
    core, group, place, across, along, opposite = places_of(groups)
    half = src.shape[-1] // 2

    def device(member_group, member):
        return (core, member_group * SPLIT + member)

    def at(distance, member):
        owner = lax.rem(group + groups - distance, groups) * SPLIT + member
        return out.at[core, owner] if both else out.at[owner]

    def part(block, which):
        return block.at[:, pl.ds(which * half, half)]

    side, line = device(group, across), device(group, along)
    twin = (1 - core, group * SPLIT + place)
    far = [lax.rem(group + k, groups) for k in range(groups)]
    greet([side, line] + [device(far[k], place) for k in range(1, groups)] + ([twin] if both else []))
    started = []

    def go(source, landing, kind, distance, target):
        copy = send(source, landing, send_sem.at[kind, distance], recv_sem.at[kind, distance], target)
        copy.start()
        started.append(copy)

    def arrive(block, kind, distance, target):
        send(block, block, send_sem.at[kind, distance], recv_sem.at[kind, distance], target).wait_recv()

    def block_for(member_group):
        return src if both else src.at[member_group]

    own = block_for(group)
    local = pltpu.make_async_copy(own, at(0, place), local_sem)
    local.start()
    go(own, at(0, place), 1, 0, side)
    go(own, at(0, place), 2, 0, line)
    for k in range(1, groups):
        go(block_for(far[k]), at(0, place), 0, k, device(far[k], place))
    if both:
        go(own, at(0, place), 5, 0, twin)
    for turn in range(groups + 2):
        k = turn
        if 0 < k < groups:
            block = at(k, place)
            arrive(block, 0, k, side)
            go(block, block, 1, k, side)
            go(block, block, 2, k, line)
            if both:
                go(block, block, 5, k, twin)
        k = turn - 1
        if 0 <= k < groups:
            block = at(k, across)
            arrive(block, 1, k, side)
            go(part(block, 0), part(block, 0), 3, k, line)
            if both:
                go(block, block, 6, k, twin)
            block = at(k, along)
            arrive(block, 2, k, line)
            go(part(block, 1), part(block, 1), 4, k, side)
            if both:
                go(block, block, 7, k, twin)
        k = turn - 2
        if 0 <= k < groups:
            block = at(k, opposite)
            arrive(part(block, 0), 3, k, line)
            arrive(part(block, 1), 4, k, side)
            if both:
                go(block, block, 8, k, twin)
    if both:
        for kind, member in ((5, place), (6, across), (7, along), (8, opposite)):
            for k in range(groups):
                owner = lax.rem(group + groups - k, groups) * SPLIT + member
                arrive(out.at[1 - core, owner], kind, k, twin)
    local.wait()
    for copy in started:
        copy.wait_send()


def spread(blocks, both, identity):
    dp_count = lax.axis_size("dp")
    groups = dp_count // SPLIT
    shape = (dp_count,) + blocks.shape[-2:]
    kinds = 9 if both else 5
    space = pl.BlockSpec(memory_space=pl.ANY if both else pltpu.VMEM)
    return pl.pallas_call(
        lambda *refs: spread_kernel(groups, both, *refs),
        out_shape=jax.ShapeDtypeStruct(((2,) if both else ()) + shape, blocks.dtype),
        in_specs=[space],
        out_specs=space,
        scratch_shapes=[
            pltpu.SemaphoreType.DMA((kinds, groups)),
            pltpu.SemaphoreType.DMA((kinds, groups)),
            pltpu.SemaphoreType.DMA,
        ],
        compiler_params=pltpu.CompilerParams(collective_id=identity, has_side_effects=True),
    )(blocks)


def collapse_kernel(groups, total, src, out, near, passed, pair, leaving, landed, send_sem, recv_sem):
    core, group, place, across, along, opposite = places_of(groups)
    half = src.shape[-1] // 2

    def device(member_group, member):
        return (core, member_group * SPLIT + member)

    side, line = device(group, across), device(group, along)
    far = [lax.rem(group + k, groups) for k in range(groups)]
    back = [lax.rem(group + groups - k, groups) for k in range(groups)]
    greet([side, line] + [device(far[k], place) for k in range(1, groups)])
    order = list(range(1, groups)) + [0]
    started = []

    def copy_of(source, landing, kind, k, target):
        return send(source, landing, send_sem.at[kind, k], recv_sem.at[kind, k], target)

    def go(*parts):
        copy = copy_of(*parts)
        copy.start()
        started.append(copy)

    wide = jnp.float32
    first, second = pl.ds(0, half), pl.ds(half, half)
    for k in order:
        block = src.at[far[k] * SPLIT + opposite]
        go(block.at[:, first], near.at[0, k], 0, k, line)
        go(block.at[:, second], near.at[1, k], 1, k, side)
    for k in order:
        index = far[k] * SPLIT + across
        copy_of(near.at[0, k], near.at[0, k], 0, k, line).wait_recv()
        passed[0, k, :, first] = (
            src[index, :, first].astype(wide) + near[0, k].astype(wide)
        ).astype(jnp.bfloat16)
        passed[0, k, :, second] = src[index, :, second]
        go(passed.at[0, k], pair.at[0, k], 2, k, side)
        index = far[k] * SPLIT + along
        copy_of(near.at[1, k], near.at[1, k], 1, k, side).wait_recv()
        passed[1, k, :, second] = (
            src[index, :, second].astype(wide) + near[1, k].astype(wide)
        ).astype(jnp.bfloat16)
        passed[1, k, :, first] = src[index, :, first]
        go(passed.at[1, k], pair.at[1, k], 3, k, line)
    for k in order:
        copy_of(pair.at[0, k], pair.at[0, k], 2, k, side).wait_recv()
        copy_of(pair.at[1, k], pair.at[1, k], 3, k, line).wait_recv()
        whole = (
            src[far[k] * SPLIT + place].astype(wide)
            + pair[0, k].astype(wide)
            + pair[1, k].astype(wide)
        )
        if k > 0:
            leaving[k] = whole.astype(jnp.bfloat16)
            go(leaving.at[k], landed.at[k], 4, k, device(far[k], place))
        elif total:
            out[...] = whole
        else:
            out[group] = whole.astype(jnp.bfloat16)
    for k in range(1, groups):
        copy_of(landed.at[k], landed.at[k], 4, k, side).wait_recv()
        if total:
            out[...] += landed[k].astype(wide)
        else:
            out[back[k]] = landed[k]
    for copy in started:
        copy.wait_send()


def collapse(blocks, total, identity):
    groups = blocks.shape[0] // SPLIT
    rows, columns = blocks.shape[1:]
    result = (
        jax.ShapeDtypeStruct((rows, columns), jnp.float32)
        if total
        else jax.ShapeDtypeStruct((groups, rows, columns), blocks.dtype)
    )
    vmem = pl.BlockSpec(memory_space=pltpu.VMEM)
    return pl.pallas_call(
        lambda *refs: collapse_kernel(groups, total, *refs),
        out_shape=result,
        in_specs=[vmem],
        out_specs=vmem,
        scratch_shapes=[
            pltpu.VMEM((2, groups, rows, columns // 2), blocks.dtype),
            pltpu.VMEM((2, groups, rows, columns), blocks.dtype),
            pltpu.VMEM((2, groups, rows, columns), blocks.dtype),
            pltpu.VMEM((groups, rows, columns), blocks.dtype),
            pltpu.VMEM((groups, rows, columns), blocks.dtype),
            pltpu.SemaphoreType.DMA((5, groups)),
            pltpu.SemaphoreType.DMA((5, groups)),
        ],
        compiler_params=pltpu.CompilerParams(
            collective_id=identity, has_side_effects=True, vmem_limit_bytes=36 << 20
        ),
    )(blocks)


def grouped_rows(select, token_rows):
    return jnp.einsum(
        "ect,td->ecd", select, token_rows, preferred_element_type=jnp.float32
    ).astype(jnp.bfloat16)


def rms_back(grad_rows, inputs, scale_rows):
    normal_rows = inputs * scale_rows
    return scale_rows * (
        grad_rows - normal_rows * jnp.mean(grad_rows * normal_rows, axis=-1, keepdims=True)
    )


def smooth(values):
    return jax.nn.gelu(values, approximate=True)


def expert_pull(hidden_rows, rows_grad, weight_in, weight_back):
    active_grad = jnp.einsum(
        "rd,fd->rf", rows_grad, weight_back, preferred_element_type=jnp.float32
    )
    smooth_pull = jax.vjp(smooth, hidden_rows)[1]
    hidden_grad = smooth_pull(active_grad)[0].astype(jnp.bfloat16)
    copy_grad = jnp.einsum(
        "rf,df->rd", hidden_grad, weight_in, preferred_element_type=jnp.float32
    ).astype(jnp.bfloat16)
    return hidden_grad, copy_grad


def layer_forward(layer_in, weights, route_now, lengths, weight_in, weight_back, upstream=None):
    gain_one, w_qkv, table, w_out, gain_two, w_route = weights
    row_count, model_width = layer_in.shape
    dp_count = lax.axis_size("dp")
    expert_count = w_route.shape[1]
    slot_count = 3 * row_count * SPLIT // (2 * dp_count)
    scale_one = lax.rsqrt(jnp.mean(layer_in * layer_in, axis=-1, keepdims=True) + EPSILON)
    normed = (layer_in * scale_one * gain_one.astype(jnp.float32)).astype(jnp.bfloat16)
    qkv_rows = jnp.dot(normed, w_qkv, preferred_element_type=jnp.float32).astype(jnp.bfloat16)
    query_heads, key_heads, value_heads = split_heads(qkv_rows)
    score_bias, bucket_picks = bias_of(table, row_count)
    same_doc = same_of(lengths, row_count)
    scores = scores_of(query_heads, key_heads, score_bias, same_doc)
    row_max = jnp.max(scores, axis=-1, keepdims=True)
    exp_rows = jnp.exp(scores - row_max)
    exp_total = jnp.sum(exp_rows, axis=-1, keepdims=True)
    soft_rows = exp_rows / exp_total
    soft_low = soft_rows.astype(jnp.bfloat16)
    attended = jnp.einsum("hts,shd->thd", soft_low, value_heads, preferred_element_type=jnp.float32)
    attended = attended.reshape(row_count, model_width).astype(jnp.bfloat16)
    middle = layer_in + jnp.dot(attended, w_out, preferred_element_type=jnp.float32)
    scale_two = lax.rsqrt(jnp.mean(middle * middle, axis=-1, keepdims=True) + EPSILON)
    routed = (middle * scale_two * gain_two.astype(jnp.float32)).astype(jnp.bfloat16)
    logits = jnp.dot(routed, w_route, preferred_element_type=jnp.float32)
    choice_prob = jax.nn.softmax(logits, axis=-1)
    picked = (route_now[:, None] == jnp.arange(expert_count, dtype=jnp.int32)[None, :]).astype(
        jnp.float32
    )
    gate_prob = jnp.sum(choice_prob * picked, axis=-1)
    select = placement_of(route_now, expert_count, slot_count)
    grouped = grouped_rows(select, routed)
    if upstream is None:
        arrived = spread(grouped, False, 1)
    else:
        down_grad = (gate_prob[:, None] * upstream).astype(jnp.bfloat16)
        grouped = jnp.concatenate([grouped, grouped_rows(select, down_grad)], axis=1)
        arrived_both = spread(grouped, False, 4)
        arrived = arrived_both[:, :slot_count]
        rows_grad = arrived_both[:, slot_count:].reshape(-1, model_width)
    token_rows = arrived.reshape(-1, model_width)
    hidden = jnp.dot(token_rows, weight_in, preferred_element_type=jnp.float32)
    active = smooth(hidden).astype(jnp.bfloat16)
    partial_out = (
        jnp.dot(active, weight_back, preferred_element_type=jnp.float32)
        .astype(jnp.bfloat16)
        .reshape(arrived.shape)
    )
    if upstream is None:
        returned = collapse(partial_out, False, 2)
        early = None
    else:
        hidden_grad, copy_grad = expert_pull(hidden, rows_grad, weight_in, weight_back)
        leaving = jnp.concatenate([partial_out, copy_grad.reshape(arrived.shape)], axis=1)
        coming = collapse(leaving, False, 5)
        returned = coming[:, :slot_count]
        early = (rows_grad, hidden_grad, coming[:, slot_count:])
    hidden = hidden.reshape(arrived.shape[0], arrived.shape[1], -1)
    combined = jnp.einsum(
        "ecd,ect->td",
        returned,
        select,
        preferred_element_type=jnp.float32,
    )
    result = middle + gate_prob[:, None] * combined
    kept_state = (
        layer_in,
        scale_one,
        normed,
        qkv_rows,
        soft_rows,
        attended,
        middle,
        scale_two,
        routed,
        choice_prob,
        gate_prob,
        combined,
        active,
        hidden,
        arrived,
        early,
    )
    return (result, kept_state)


def layer_backward(upstream, kept_state, weights, route_now, lengths, weight_in, weight_back):
    (
        layer_in,
        scale_one,
        normed,
        qkv_rows,
        soft_rows,
        attended,
        middle,
        scale_two,
        routed,
        choice_prob,
        gate_prob,
        combined,
        active,
        hidden,
        arrived,
        early,
    ) = kept_state
    gain_one, w_qkv, table, w_out, gain_two, w_route = weights
    row_count, model_width = layer_in.shape
    dp_count = lax.axis_size("dp")
    expert_count = w_route.shape[1]
    slot_count = 3 * row_count * SPLIT // (2 * dp_count)
    picked = (route_now[:, None] == jnp.arange(expert_count, dtype=jnp.int32)[None, :]).astype(
        jnp.float32
    )
    select = placement_of(route_now, expert_count, slot_count)
    gate_grad = jnp.sum(upstream * combined, axis=-1)
    logit_grad = (choice_prob * (picked - gate_prob[:, None]) * gate_grad[:, None]).astype(
        jnp.bfloat16
    )
    routed_grad = jnp.einsum("te,de->td", logit_grad, w_route, preferred_element_type=jnp.float32)
    if early is None:
        down_grad = (gate_prob[:, None] * upstream).astype(jnp.bfloat16)
        rows_grad = spread(grouped_rows(select, down_grad), False, 1).reshape(-1, model_width)
        hidden_rows = hidden.reshape(rows_grad.shape[0], -1)
        hidden_grad, copy_grad = expert_pull(hidden_rows, rows_grad, weight_in, weight_back)
        copy_back = collapse(copy_grad.reshape(dp_count, slot_count, model_width), False, 2)
    else:
        rows_grad, hidden_grad, copy_back = early
    arrived_rows = arrived.reshape(-1, model_width)
    routed_grad = routed_grad + jnp.einsum(
        "ecd,ect->td",
        copy_back,
        select,
        preferred_element_type=jnp.float32,
    )
    gain_two_grad = jnp.sum(routed_grad * middle * scale_two, axis=0)
    middle_grad = upstream + rms_back(routed_grad * gain_two.astype(jnp.float32), middle, scale_two)
    branch_grad = middle_grad.astype(jnp.bfloat16)
    attended_grad = jnp.einsum(
        "te,de->td", branch_grad, w_out, preferred_element_type=jnp.float32
    ).astype(jnp.bfloat16)
    attended_grad = attended_grad.reshape(row_count, HEADS, HD)
    query_heads, key_heads, value_heads = split_heads(qkv_rows)
    bucket_picks = picks_of(row_count)
    value_grad = jnp.einsum(
        "hts,thd->shd",
        soft_rows.astype(jnp.bfloat16),
        attended_grad,
        preferred_element_type=jnp.float32,
    )
    prob_grad = jnp.einsum(
        "thd,shd->hts", attended_grad, value_heads, preferred_element_type=jnp.float32
    )
    score_grad = (
        soft_rows * (prob_grad - jnp.sum(soft_rows * prob_grad, axis=-1, keepdims=True))
    ).astype(jnp.bfloat16)
    query_grad = jnp.einsum(
        "hts,shd->thd", score_grad, key_heads, preferred_element_type=jnp.float32
    ) * (1.0 / math.sqrt(HD))
    key_grad = jnp.einsum(
        "hts,thd->shd", score_grad, query_heads, preferred_element_type=jnp.float32
    ) * (1.0 / math.sqrt(HD))
    table_grad = jnp.einsum(
        "tsb,hts->bh", bucket_picks, score_grad, preferred_element_type=jnp.float32
    ).reshape(-1)
    qkv_grad = jnp.concatenate(
        [
            query_grad.reshape(row_count, model_width),
            key_grad.reshape(row_count, model_width),
            value_grad.reshape(row_count, model_width),
        ],
        axis=1,
    ).astype(jnp.bfloat16)
    normed_grad = jnp.einsum("te,de->td", qkv_grad, w_qkv, preferred_element_type=jnp.float32)
    gain_one_grad = jnp.sum(normed_grad * layer_in * scale_one, axis=0)
    input_grad = middle_grad + rms_back(
        normed_grad * gain_one.astype(jnp.float32), layer_in, scale_one
    )
    small_grads = (gain_one_grad, table_grad, gain_two_grad)
    factor_rows = (normed, qkv_grad, attended, branch_grad, routed, logit_grad)
    expert_rows = (arrived_rows, hidden_grad, active, rows_grad)
    return (input_grad, small_grads, factor_rows, expert_rows)


def shared_from(small_grads, factor_rows):
    normed, qkv_grad, attended, branch_grad, routed, logit_grad = factor_rows
    qkv_weight_grad = jnp.einsum("td,te->de", normed, qkv_grad, preferred_element_type=jnp.float32)
    out_weight_grad = jnp.einsum(
        "td,te->de", attended, branch_grad, preferred_element_type=jnp.float32
    )
    route_weight_grad = jnp.einsum(
        "td,te->de", routed, logit_grad, preferred_element_type=jnp.float32
    )
    return (
        small_grads[0],
        qkv_weight_grad,
        small_grads[1],
        out_weight_grad,
        small_grads[2],
        route_weight_grad,
    )


SMALL = 256


def swap_cores(block):
    return lax.ppermute(block, "section", [(0, 1), (1, 0)])


def per_core(section_index, first_one, second_one):
    return jnp.where(section_index == 0, first_one, second_one)


def pack_columns(wide, square, columns):
    small = jnp.concatenate(columns, axis=1)
    small = jnp.pad(small, ((0, 0), (0, SMALL - small.shape[1])))
    return jnp.concatenate([wide, square, small], axis=1)


def spaced(table, group_count):
    table = table.reshape(group_count, -1)
    row_share = 2 * table.shape[1]
    return jnp.pad(table, ((0, 0), (0, row_share - table.shape[1]))).reshape(-1, 1)


def unpack_weights(packed, width, expert_count):
    dp_count = lax.axis_size("dp")
    small = packed[:, 4 * width :]
    table = small[:, 2].reshape(dp_count, -1)
    table = table[:, : table.shape[1] // 2].reshape(-1)
    return (
        small[:, 0],
        packed[:, : 3 * width],
        table,
        packed[:, 3 * width : 4 * width],
        small[:, 1],
        small[:, 3 : 3 + expert_count],
    )


def shards(
    tokens,
    out_grad,
    routes,
    doc_lengths,
    norm_attn,
    attn_qkv,
    rel_bias,
    attn_out,
    norm_ffn,
    router,
    expert_in,
    expert_out,
):
    core = lax.axis_index("section")
    dp_count = lax.axis_size("dp")
    width = tokens.shape[2]
    expert_count = router.shape[2]
    own_pack = pack_columns(
        attn_qkv[0],
        attn_out[0],
        [norm_attn[0][:, None], norm_ffn[0][:, None], spaced(rel_bias[0], 1), router[0]],
    )
    packs = spread(own_pack, True, 0)
    weights = [
        unpack_weights(packs[layer].reshape(width, own_pack.shape[1]), width, expert_count)
        for layer in range(2)
    ]
    other_in = swap_cores(expert_in[0, 0])
    other_out = swap_cores(expert_out[0, 0])
    ins = [per_core(core, expert_in[0, 0], other_in), per_core(core, other_in, expert_in[0, 0])]
    outs = [
        per_core(core, expert_out[0, 0], other_out),
        per_core(core, other_out, expert_out[0, 0]),
    ]
    route_table = routes[0, :, :, 0]
    other_route = swap_cores(per_core(core, route_table[1], route_table[0]))
    own_route = per_core(core, route_table[0], route_table[1])
    route_rows = [
        per_core(core, own_route, other_route),
        per_core(core, other_route, own_route),
    ]
    lengths = per_core(core, doc_lengths[0, 0], doc_lengths[1, 0])
    layer_in = per_core(core, tokens[0], tokens[1]).astype(jnp.float32)
    upstream = per_core(core, out_grad[0], out_grad[1]).astype(jnp.float32)
    kept, lows = [], []
    for layer in range(2):
        result, state = layer_forward(
            layer_in,
            weights[layer],
            route_rows[layer],
            lengths,
            ins[layer],
            outs[layer],
            upstream if layer == 1 else None,
        )
        low = result.astype(jnp.bfloat16)
        lows.append(low)
        kept.append(state)
        layer_in = low.astype(jnp.float32)

    def sorted_out(pair):
        mine = per_core(core, pair[0], pair[1])
        theirs = swap_cores(per_core(core, pair[1], pair[0]))
        return jnp.stack([per_core(core, mine, theirs), per_core(core, theirs, mine)])

    input_grads, expert_rows = [None, None], [None, None]
    factors, smalls = [None, None], [None, None]
    for layer in (1, 0):
        input_grad, smalls[layer], factors[layer], expert_rows[layer] = layer_backward(
            upstream,
            kept[layer],
            weights[layer],
            route_rows[layer],
            lengths,
            ins[layer],
            outs[layer],
        )
        input_grads[layer] = input_grad
        upstream = input_grad.astype(jnp.bfloat16).astype(jnp.float32)

    def own_layer(pair):
        mine = per_core(core, pair[0], pair[1])
        return mine, swap_cores(per_core(core, pair[1], pair[0]))

    joined = own_layer([jnp.concatenate(group, axis=1) for group in factors])
    joined = jnp.concatenate(joined, axis=0)
    ends = np.cumsum([member.shape[1] for member in factors[0]])
    factor_rows = [
        joined[:, end - member.shape[1] : end] for end, member in zip(ends, factors[0])
    ]
    small_pair = own_layer([jnp.concatenate(group, axis=0) for group in smalls])
    small_sum = small_pair[0] + small_pair[1]
    small_grads = (
        small_sum[:width],
        small_sum[width:-width],
        small_sum[-width:],
    )
    totals = shared_from(small_grads, factor_rows)
    packed = pack_columns(
        totals[1],
        totals[3],
        [totals[0][:, None], totals[4][:, None], spaced(totals[2], dp_count), totals[5]],
    ).astype(jnp.bfloat16)
    total = collapse(packed.reshape(dp_count, -1, packed.shape[1]), True, 3)

    def joined_rows(index):
        mine = per_core(core, expert_rows[0][index], expert_rows[1][index])
        theirs = swap_cores(per_core(core, expert_rows[1][index], expert_rows[0][index]))
        return jnp.concatenate([mine, theirs], axis=0)

    arrived_all, hidden_grad_all, active_all, rows_grad_all = [joined_rows(i) for i in range(4)]
    in_total = jnp.einsum(
        "rd,rf->df", arrived_all, hidden_grad_all, preferred_element_type=jnp.float32
    )
    back_total = jnp.einsum(
        "rf,rd->fd", active_all, rows_grad_all, preferred_element_type=jnp.float32
    )
    outputs = sorted_out(lows)
    input_store = sorted_out(input_grads)
    small = total[:, 4 * width :]
    return (
        outputs[None],
        input_store[None],
        small[None, :, 0],
        total[None, :, : 3 * width],
        small[None, : rel_bias.shape[1], 2],
        total[None, :, 3 * width : 4 * width],
        small[None, :, 1],
        small[None, :, 3 : 3 + expert_count],
        in_total[None, None],
        back_total[None, None],
    )


def solution(mesh):
    placed = (
        P(None, "dp", None),
        P(None, "dp", None),
        P("section", None, "dp", None),
        P(None, "dp", None),
        P("section", "dp"),
        P("section", "dp", None),
        P("section", "dp"),
        P("section", "dp", None),
        P("section", "dp"),
        P("section", "dp", None),
        P("section", "dp", None, None),
        P("section", "dp", None, None),
    )
    return jax.shard_map(
        shards,
        mesh=mesh,
        in_specs=placed,
        out_specs=(
            P("section", None, "dp", None),
            P("section", None, "dp", None),
            P("section", "dp"),
            P("section", "dp", None),
            P("section", "dp"),
            P("section", "dp", None),
            P("section", "dp"),
            P("section", "dp", None),
            P("section", "dp", None, None),
            P("section", "dp", None, None),
        ),
        check_vma=False,
    )
```
